256 devices in a mesh: tm: 64 (over z_hi, y, x), inp: 4 (over z_lo, core).
Axes of the slice: x: 4, y: 4, z: 8 (z_hi: 4, z_lo: 2; z = z_hi * 2 + z_lo), core: 2. Of those that a mesh axis runs over, the one named last changes fastest.
Arguments:
- samples: bfloat16 [1024, 262144], P('inp', 'tm'), may hold values from -6 to 6
- coeffs: float32 [16, 2048], replicated, may hold values from -1.5 to 1.5
- delays: float32 [512, 1024], replicated, may hold values from -32 to 32
Outputs:
- beams: bfloat16 [2, 1024, 512, 128], P(None, ('tm', 'inp'))
The draws below stay inside these ranges and needn't reach their ends.
All inputs are finite; a program needn't handle non-finite values.
Results may differ from the reference program's by a relative error of at most 0.015.
Values may be sent and summed in bfloat16 or wider, within the bound.
No kernel may reach another device: no remote copies, remote signals or barrier semaphores. Data moves between devices by JAX's collectives and lax.ppermute only.
A program may use at most 128 MiB of HBM per device.

```python
import math
import jax
import jax.numpy as jnp
from jax import lax

CHAN = 1024
FRAME = 2048
TAPS = 16
INPUTS = 1024
BEAMS = 512
FRAMES = 128
SAMPLES = 262144


def steps_of(rng, shape, pieces, smallest, top_value):
    def one(position, parts):
        heights = jax.random.uniform(jax.random.fold_in(jax.random.fold_in(rng, 6), position), (parts,), jnp.float32, smallest / len(pieces), top_value / len(pieces))
        return jnp.repeat(jnp.exp(heights), shape[position] // parts).reshape((-1,) + (1,) * (len(shape) - position - 1))

    gain = one(*pieces[0])
    for cut in pieces[1:]:
        gain = gain * one(*cut)
    return gain


def gaussian(own_key, dims, scale, bound, cuts=(), kind=jnp.bfloat16):
    factor_of = steps_of(own_key, dims, cuts, -0.22, 0.18) if cuts else 1.0
    values = jax.random.normal(own_key, dims, jnp.float32) * scale * factor_of
    return jnp.minimum(jnp.maximum(values, -bound), bound).astype(kind)


def setup_inputs(seed: int = 0) -> dict:
    streams_of = jax.random.split(jax.random.key(seed), 4)
    samples = gaussian(streams_of[0], (INPUTS, SAMPLES), 1.0, 6.0, ((0, 4), (1, 64)))
    coeffs = gaussian(streams_of[1], (TAPS, FRAME), TAPS ** -0.5, 1.5, (), jnp.float32)
    delays = jnp.clip(jax.random.uniform(streams_of[2], (BEAMS, INPUTS), jnp.float32, -32.0, 32.0), -32.0, 32.0)
    return dict(samples=samples, coeffs=coeffs, delays=delays)


def filter_block(block, coeffs):
    count = block.shape[0]
    frames = block.reshape(count, FRAMES, FRAME).astype(jnp.float32)
    padded = jnp.concatenate([jnp.zeros((count, TAPS - 1, FRAME), jnp.float32), frames], axis=1)
    filtered = jnp.zeros((count, FRAMES, FRAME), jnp.float32)
    for tap in range(TAPS):
        filtered = filtered + coeffs[tap] * padded[:, TAPS - 1 - tap:TAPS - 1 - tap + FRAMES]
    filtered = filtered.astype(jnp.bfloat16).astype(jnp.float32)
    spectrum = jnp.fft.rfft(filtered, axis=-1)[..., :CHAN] * (1.0 / math.sqrt(FRAME))
    return (jnp.real(spectrum).astype(jnp.bfloat16), jnp.imag(spectrum).astype(jnp.bfloat16))

def reference(samples, coeffs, delays):
    width = math.gcd(INPUTS, 64)
    blocks = samples.reshape(INPUTS // width, width, SAMPLES)
    spec_re, spec_im = lax.map(lambda block: filter_block(block, coeffs), blocks)
    spec_re = jnp.transpose(spec_re.reshape(INPUTS, FRAMES, CHAN), (2, 0, 1))
    spec_im = jnp.transpose(spec_im.reshape(INPUTS, FRAMES, CHAN), (2, 0, 1))
    factor = 2.0 * math.pi / FRAME
    scale = 1.0 / math.sqrt(INPUTS)

    def one_channel(packed):
        channel, part_re, part_im = packed
        angle = channel.astype(jnp.float32) * delays * factor
        weight_re = jnp.cos(angle).astype(jnp.bfloat16).astype(jnp.float32)
        weight_im = (-jnp.sin(angle)).astype(jnp.bfloat16).astype(jnp.float32)
        part_re = part_re.astype(jnp.float32)
        part_im = part_im.astype(jnp.float32)
        out_re = jnp.dot(weight_re, part_re, preferred_element_type=jnp.float32) - jnp.dot(weight_im, part_im, preferred_element_type=jnp.float32)
        out_im = jnp.dot(weight_re, part_im, preferred_element_type=jnp.float32) + jnp.dot(weight_im, part_re, preferred_element_type=jnp.float32)
        return (jnp.stack([out_re, out_im]) * scale).astype(jnp.bfloat16)
    formed = lax.map(one_channel, (jnp.arange(CHAN, dtype=jnp.int32), spec_re, spec_im))
    return jnp.transpose(formed, (1, 0, 2, 3))
```

```python
import math

import jax
import jax.numpy as jnp
import numpy as np
from jax import lax
from jax.experimental import pallas as pl
from jax.experimental.pallas import tpu as pltpu
from jax.sharding import Mesh
from jax.sharding import PartitionSpec as P

CHAN = 1024
FRAME = 2048
TAPS = 16
INPUTS = 1024
BEAMS = 512
FRAMES = 128

ZH, YX, INP, DEVICES = 4, 16, 4, 256
PLANE = FRAMES // ZH
LATE = 8
EARLY = TAPS - 1 - LATE
ROWS = INPUTS // INP // YX
OWN = CHAN // DEVICES
PLACES = YX * INP
LANES = 128
ALL = ("zh", "y", "x", "zl", "core")


def dft_table():
    turn = np.arange(FRAME) * (2.0 * np.pi / FRAME)
    index = np.outer(np.arange(CHAN), np.arange(FRAME)) % FRAME
    table = np.stack([np.cos(turn)[index], -np.sin(turn)[index]], axis=1)
    return table.reshape(2 * CHAN, FRAME).astype(jnp.bfloat16)


def spectra_kernel(keep_ref, prev_ref, own_ref, next_ref, coeffs_ref, table_ref, out_ref, filtered, turned):
    rows = own_ref.shape[1]

    @pl.when(pl.program_id(0) == 0)
    def _():
        keep = keep_ref[0]

        def tile(step, carry):
            lanes = pl.ds(pl.multiple_of(step * LANES, LANES), LANES)
            frames = [prev_ref[k, :, lanes] for k in range(EARLY)]
            frames += [own_ref[k, :, lanes] for k in range(PLANE)]
            frames += [next_ref[k, :, lanes] for k in range(LATE)]
            frames = [value.astype(jnp.float32) for value in frames]
            taps = [coeffs_ref[t : t + 1, lanes] for t in range(TAPS)]
            for j in range(PLANE):
                newest = TAPS - 1 + j
                wrapped = max(0, j - (PLANE - LATE) + 1)
                near = min(wrapped, TAPS) if wrapped else TAPS
                total = taps[0] * frames[newest]
                for t in range(1, near):
                    total = total + taps[t] * frames[newest - t]
                if near < TAPS:
                    old = taps[near] * frames[newest - near]
                    for t in range(near + 1, TAPS):
                        old = old + taps[t] * frames[newest - t]
                    total = total + keep * old
                turned[pl.ds(j, rows, stride=PLANE), :] = total
            filtered[:, lanes] = turned[...].astype(jnp.bfloat16)
            return carry

        lax.fori_loop(0, FRAME // LANES, tile, 0)

    spectrum = lax.dot_general(
        table_ref[...], filtered[...], (((1,), (1,)), ((), ())), preferred_element_type=jnp.float32
    )
    out_ref[...] = (spectrum * (1.0 / math.sqrt(FRAME))).astype(jnp.bfloat16)


def spectra(keep, prev, own, following, coeffs, table):
    rows = own.shape[1]
    block = 256
    whole = lambda shape: pl.BlockSpec(shape, lambda i: (0,) * len(shape))
    return pl.pallas_call(
        spectra_kernel,
        grid=(2 * CHAN // block,),
        in_specs=[
            pl.BlockSpec(memory_space=pltpu.SMEM),
            whole(prev.shape),
            whole(own.shape),
            whole(following.shape),
            whole(coeffs.shape),
            pl.BlockSpec((block, FRAME), lambda i: (i, 0)),
        ],
        out_specs=pl.BlockSpec((block, rows * PLANE), lambda i: (i, 0)),
        out_shape=jax.ShapeDtypeStruct((2 * CHAN, rows * PLANE), jnp.bfloat16),
        scratch_shapes=[
            pltpu.VMEM((rows * PLANE, FRAME), jnp.bfloat16),
            pltpu.VMEM((rows * PLANE, LANES), jnp.float32),
        ],
        compiler_params=pltpu.CompilerParams(vmem_limit_bytes=40 << 20),
        cost_estimate=pl.CostEstimate(
            flops=2 * 2 * CHAN * FRAME * rows * PLANE, bytes_accessed=14 << 20, transcendentals=0
        ),
    )(keep, prev, own, following, coeffs, table)


def fit(values):
    nodes = (np.cos(np.pi * (np.arange(64) + 0.5) / 64) + 1.0) / 8.0
    return [float(v) for v in np.polynomial.Polynomial.fit(nodes, values(np.sqrt(nodes)), 7, domain=[0, 0.25], window=[0, 0.25]).coef]


COS = fit(lambda r: np.cos(2 * np.pi * r))
SIN = fit(lambda r: np.sin(2 * np.pi * r) / r)


def cos_sin(turns):
    rest = turns - jnp.round(turns)
    square = rest * rest
    cos, sin = COS[-1], SIN[-1]
    for a, b in zip(COS[-2::-1], SIN[-2::-1]):
        cos = cos * square + a
        sin = sin * square + b
    return cos, sin * rest


def weights_kernel(first_ref, delays_ref, out_ref):
    delay = delays_ref[...] * (1.0 / FRAME)
    step_cos, step_sin = cos_sin(delay)
    cos, sin = cos_sin(delay * first_ref[0])
    for c in range(OWN):
        if c:
            cos, sin = cos * step_cos - sin * step_sin, sin * step_cos + cos * step_sin
        out_ref[c, 0] = cos.astype(jnp.bfloat16)
        out_ref[c, 1] = (-sin).astype(jnp.bfloat16)


def weights(first, delays):
    block = 64
    return pl.pallas_call(
        weights_kernel,
        grid=(BEAMS // block,),
        in_specs=[
            pl.BlockSpec(memory_space=pltpu.SMEM),
            pl.BlockSpec((block, INPUTS), lambda i: (i, 0)),
        ],
        out_specs=pl.BlockSpec((OWN, 2, block, INPUTS), lambda i: (0, 0, i, 0)),
        out_shape=jax.ShapeDtypeStruct((OWN, 2, BEAMS, INPUTS), jnp.bfloat16),
        compiler_params=pltpu.CompilerParams(vmem_limit_bytes=24 << 20),
        cost_estimate=pl.CostEstimate(
            flops=60 * BEAMS * INPUTS, bytes_accessed=10 << 20, transcendentals=0
        ),
    )(first, delays)


def beams_kernel(spectra_ref, weights_ref, out_ref, wide, values):
    tiles = spectra_ref.shape[2] // LANES
    group = LANES // PLANE
    channel = pl.program_id(0)

    @pl.when(channel == 0)
    def _():
        lane = lax.broadcasted_iota(jnp.int32, (PLACES, LANES), 1)
        low = lane < 2 * PLANE
        even = lax.rem(lane, 2 * PLANE) < PLANE
        for tile in range(tiles):
            part = spectra_ref[:, :, tile * LANES : (tile + 1) * LANES]
            wide[...] = part.astype(jnp.float32).reshape(DEVICES * 2 * OWN, LANES)
            for own in range(OWN):
                for side in range(2):
                    a = [
                        wide[pl.ds(zh * PLACES * 2 * OWN + 2 * own + side, PLACES, stride=2 * OWN), :]
                        for zh in range(ZH)
                    ]
                    half = 2 * PLANE
                    low_a = jnp.where(low, a[0], pltpu.roll(a[2], half, 1))
                    low_b = jnp.where(low, a[1], pltpu.roll(a[3], half, 1))
                    high_a = jnp.where(low, pltpu.roll(a[0], half, 1), a[2])
                    high_b = jnp.where(low, pltpu.roll(a[1], half, 1), a[3])
                    b = [
                        jnp.where(even, low_a, pltpu.roll(low_b, PLANE, 1)),
                        jnp.where(even, pltpu.roll(low_a, LANES - PLANE, 1), low_b),
                        jnp.where(even, high_a, pltpu.roll(high_b, PLANE, 1)),
                        jnp.where(even, pltpu.roll(high_a, LANES - PLANE, 1), high_b),
                    ]
                    for k in range(group):
                        at = (tile * group + k) * PLACES
                        values[own, at : at + PLACES, side * LANES : (side + 1) * LANES] = b[k].astype(
                            jnp.bfloat16
                        )

    here = values[channel]
    by_re = jnp.dot(weights_ref[0, 0], here, preferred_element_type=jnp.float32)
    by_im = jnp.dot(weights_ref[0, 1], here, preferred_element_type=jnp.float32)
    out_re = (by_re[:, :LANES] - by_im[:, LANES:]) * (1.0 / math.sqrt(INPUTS))
    out_im = (by_re[:, LANES:] + by_im[:, :LANES]) * (1.0 / math.sqrt(INPUTS))
    out_ref[0, 0] = pltpu.roll(out_re, LATE, 1).astype(jnp.bfloat16)
    out_ref[1, 0] = pltpu.roll(out_im, LATE, 1).astype(jnp.bfloat16)


def beams(received, weight):
    return pl.pallas_call(
        beams_kernel,
        grid=(OWN,),
        in_specs=[
            pl.BlockSpec(received.shape, lambda i: (0, 0, 0)),
            pl.BlockSpec((1, 2, BEAMS, INPUTS), lambda i: (i, 0, 0, 0)),
        ],
        out_specs=pl.BlockSpec((2, 1, BEAMS, FRAMES), lambda i: (0, i, 0, 0)),
        out_shape=jax.ShapeDtypeStruct((2, OWN, BEAMS, FRAMES), jnp.bfloat16),
        scratch_shapes=[
            pltpu.VMEM((DEVICES * 2 * OWN, LANES), jnp.float32),
            pltpu.VMEM((OWN, INPUTS, 2 * LANES), jnp.bfloat16),
        ],
        compiler_params=pltpu.CompilerParams(vmem_limit_bytes=40 << 20),
        cost_estimate=pl.CostEstimate(
            flops=8 * OWN * BEAMS * INPUTS * FRAMES, bytes_accessed=11 << 20, transcendentals=0
        ),
    )(received, weight)


def body(samples, coeffs, delays):
    zh = lax.axis_index("zh")
    first = (lax.axis_index(ALL) * OWN).astype(jnp.float32).reshape(1)
    keep = jnp.where(zh == ZH - 1, 0.0, 1.0).astype(jnp.float32).reshape(1)
    table = jnp.asarray(dft_table())

    ordered = delays.reshape(BEAMS, INP, YX, ROWS).transpose(0, 3, 2, 1).reshape(BEAMS, INPUTS)
    weight = weights(first, ordered)

    own = lax.all_to_all(samples.reshape(YX, ROWS, 2 * FRAME), ("y", "x"), 0, 0, tiled=True)
    own = own.reshape(YX, ROWS, 2, FRAME).transpose(0, 2, 1, 3).reshape(PLANE, ROWS, FRAME)
    prev = lax.ppermute(own[PLANE - EARLY :], "zh", [(i, i + 1) for i in range(ZH - 1)])
    following = lax.ppermute(own[:LATE], "zh", [(i, (i - 1) % ZH) for i in range(ZH)])
    spectrum = spectra(keep, prev, own, following, coeffs, table)
    blocks = spectrum.reshape(DEVICES, 2 * OWN, ROWS * PLANE)
    received = lax.all_to_all(blocks, ALL, 0, 0, tiled=True)
    return beams(received, weight)


def solution(mesh):
    fine = Mesh(mesh.devices.reshape(4, 4, 4, 2, 2), ALL)
    in_specs = (P(("zl", "core"), ("zh", "y", "x")), P(), P())
    out_specs = P(None, ALL, None, None)
    return jax.shard_map(body, mesh=fine, in_specs=in_specs, out_specs=out_specs, check_vma=False)
```

```python
import math

import jax
import jax.numpy as jnp
import numpy as np
from jax import lax
from jax.experimental import pallas as pl
from jax.experimental.pallas import tpu as pltpu
from jax.sharding import Mesh
from jax.sharding import PartitionSpec as P

CHAN = 1024
FRAME = 2048
TAPS = 16
INPUTS = 1024
BEAMS = 512
FRAMES = 128

ZH, YX, INP, DEVICES = 4, 16, 4, 256
PLANE = FRAMES // ZH
LATE = 8
HALO = LATE // 2
CHUNKS = 2
ROWS = INPUTS // INP // YX // CHUNKS
OWN = CHAN // DEVICES
PLACES = YX * INP
LANES = 128
ALL = ("zh", "y", "x", "zl", "core")


def dft_tables():
    turn = np.arange(FRAME) * (2.0 * np.pi / FRAME)
    index = np.outer(np.arange(CHAN), np.arange(FRAME // 2)) % FRAME
    table = np.stack([np.cos(turn)[index], -np.sin(turn)[index]], axis=1)
    table = table.reshape(CHAN // 2, 2, 2, FRAME // 2).transpose(1, 0, 2, 3)
    return table.reshape(2, CHAN, FRAME // 2).astype(jnp.bfloat16)


def filter_frames(frame, taps, turned, keep):
    frames = [frame(k) for k in range(PLANE + TAPS - 1)]
    for j in range(PLANE):
        newest = TAPS - 1 + j
        near = j - (PLANE - LATE) + 1
        near = near if near > 0 else TAPS
        total = taps[0] * frames[newest]
        for t in range(1, near):
            total = total + taps[t] * frames[newest - t]
        if near < TAPS:
            old = taps[near] * frames[newest - near]
            for t in range(near + 1, TAPS):
                old = old + taps[t] * frames[newest - t]
            total = total + keep * old
        turned[pl.ds(j, ROWS, stride=PLANE), :] = total


def resident(value):
    return pltpu.with_memory_space_constraint(value, pltpu.VMEM)


def spectra_kernel(chunk, keep_ref, prev_ref, own_ref, next_ref, coeffs_ref, table_ref, *refs):
    out_ref, tables, sums, turned, result, table_sems, out_sems = refs[min(chunk, 1) :]
    steps = out_sems.shape[0]
    block = CHAN // steps
    width = ROWS * PLANE

    def table_copy(step):
        cut = pl.ds(step * block, block)
        return pltpu.make_async_copy(table_ref.at[:, cut], tables.at[:, cut], table_sems.at[step])

    def out_copy(step):
        cut = pl.ds(step * block // 4, block // 4)
        lanes = pl.ds(chunk * width, width)
        return pltpu.make_async_copy(result.at[cut], out_ref.at[cut, :, lanes], out_sems.at[step])

    for step in range(steps):
        table_copy(step).start()

    def tile(step, carry):
        for side in range(2):
            base = pl.multiple_of(step * LANES, LANES) + side * (FRAME // 2)

            def frame(k):
                k += 1
                ref = prev_ref if k < LATE else own_ref if k < LATE + PLANE else next_ref
                k = k if k < LATE else k - LATE if k < LATE + PLANE else k - LATE - PLANE
                return ref[k // 2, :, pl.ds(base + (k % 2) * FRAME, LANES)].astype(jnp.float32)

            taps = [coeffs_ref[t : t + 1, pl.ds(base, LANES)] for t in range(TAPS)]
            filter_frames(frame, taps, turned.at[side], keep_ref[0])
        lanes = pl.ds(pl.multiple_of(step * LANES, LANES), LANES)
        first, second = turned[0], turned[1]
        sums[0, :, lanes] = (first + second).astype(jnp.bfloat16)
        sums[1, :, lanes] = (first - second).astype(jnp.bfloat16)
        return carry

    lax.fori_loop(0, FRAME // 2 // LANES, tile, 0)

    upper = lax.broadcasted_iota(jnp.int32, (block // 8, 8, width), 1) < 4
    for step in range(steps):
        table_copy(step).wait()
        cut = slice(step * block, (step + 1) * block)
        even, odd = (
            lax.dot_general(
                tables[k, cut], sums[k], (((1,), (1,)), ((), ())), preferred_element_type=jnp.float32
            ).reshape(block // 8, 8, width)
            * (1.0 / math.sqrt(FRAME))
            for k in range(2)
        )
        one = jnp.where(upper, even, pltpu.roll(odd, 4, 1)).astype(jnp.bfloat16)
        two = jnp.where(upper, pltpu.roll(even, 4, 1), odd).astype(jnp.bfloat16)
        for k in range(block // 8):
            result[step * block // 4 + 2 * k] = one[k]
            result[step * block // 4 + 2 * k + 1] = two[k]
        out_copy(step).start()
    for step in range(steps):
        out_copy(step).wait()


def spectra(chunk, keep, prev, own, following, coeffs, table, earlier=()):
    steps = 4
    vmem = pl.BlockSpec(memory_space=pltpu.VMEM)
    hbm = pl.BlockSpec(memory_space=pl.ANY)
    return pl.pallas_call(
        lambda *refs: spectra_kernel(chunk, *refs),
        in_specs=[pl.BlockSpec(memory_space=pltpu.SMEM)] + [vmem] * 4 + [hbm] + [hbm] * len(earlier),
        out_specs=hbm,
        out_shape=jax.ShapeDtypeStruct((DEVICES, 2 * OWN, CHUNKS * ROWS * PLANE), jnp.bfloat16),
        scratch_shapes=[
            pltpu.VMEM(table.shape, jnp.bfloat16),
            pltpu.VMEM((2, ROWS * PLANE, FRAME // 2), jnp.bfloat16),
            pltpu.VMEM((2, ROWS * PLANE, LANES), jnp.float32),
            pltpu.VMEM((DEVICES, 2 * OWN, ROWS * PLANE), jnp.bfloat16),
            pltpu.SemaphoreType.DMA((steps,)),
            pltpu.SemaphoreType.DMA((steps,)),
        ],
        input_output_aliases={6: 0} if earlier else {},
        compiler_params=pltpu.CompilerParams(vmem_limit_bytes=20 << 20),
        cost_estimate=pl.CostEstimate(
            flops=2 * CHAN * FRAME * ROWS * PLANE, bytes_accessed=7 << 20, transcendentals=0
        ),
    )(keep, prev, own, following, coeffs, table, *earlier)


def fit(values):
    nodes = (np.cos(np.pi * (np.arange(64) + 0.5) / 64) + 1.0) / 8.0
    return [float(v) for v in np.polynomial.Polynomial.fit(nodes, values(np.sqrt(nodes)), 7, domain=[0, 0.25], window=[0, 0.25]).coef]


COS = fit(lambda r: np.cos(2 * np.pi * r))
SIN = fit(lambda r: np.sin(2 * np.pi * r) / r)


def cos_sin(turns):
    rest = turns - jnp.round(turns)
    square = rest * rest
    cos, sin = COS[-1], SIN[-1]
    for a, b in zip(COS[-2::-1], SIN[-2::-1]):
        cos = cos * square + a
        sin = sin * square + b
    return cos, sin * rest


def weights_kernel(first_ref, delays_ref, out_ref):
    block = 16

    def rows(step, carry):
        at = pl.ds(pl.multiple_of(step * block, block), block)
        delay = delays_ref[at] * (1.0 / FRAME)
        step_cos, step_sin = cos_sin(delay)
        cos, sin = cos_sin(delay * first_ref[0])
        for c in range(OWN):
            if c:
                cos, sin = cos * step_cos - sin * step_sin, sin * step_cos + cos * step_sin
            out_ref[c, 0, at] = cos.astype(jnp.bfloat16)
            out_ref[c, 1, at] = (-sin).astype(jnp.bfloat16)
        return carry

    lax.fori_loop(0, BEAMS // block, rows, 0)


def weights(first, delays):
    return pl.pallas_call(
        weights_kernel,
        in_specs=[pl.BlockSpec(memory_space=pltpu.SMEM), pl.BlockSpec(memory_space=pltpu.VMEM)],
        out_specs=pl.BlockSpec(memory_space=pltpu.VMEM),
        out_shape=pltpu.VMEM((OWN, 2, BEAMS, INPUTS), jnp.bfloat16),
        compiler_params=pltpu.CompilerParams(vmem_limit_bytes=14 << 20),
        cost_estimate=pl.CostEstimate(
            flops=60 * BEAMS * INPUTS, bytes_accessed=10 << 20, transcendentals=0
        ),
    )(first, delays)


def arrange(spectra_ref, wide, values):
    lane = lax.broadcasted_iota(jnp.int32, (PLACES, LANES), 1)
    rows = 2 * OWN
    for tile in range(spectra_ref.shape[2] // LANES):
        part = spectra_ref[:, :, tile * LANES : (tile + 1) * LANES]
        wide[...] = part.astype(jnp.float32).reshape(DEVICES * rows, LANES)
        for own in range(OWN):
            for side in range(2):
                row = 4 * (own % 2) + 2 * (own // 2) + side
                a = [wide[pl.ds(zh * PLACES * rows + row, PLACES, stride=rows), :] for zh in range(ZH)]
                for bit in (2, 1):
                    size = bit * PLANE
                    keep = lax.rem(lane, 2 * size) < size
                    for k in range(ZH):
                        if not k & bit:
                            x, y = a[k], a[k + bit]
                            a[k] = jnp.where(keep, x, pltpu.roll(y, size, 1))
                            a[k + bit] = jnp.where(keep, pltpu.roll(x, LANES - size, 1), y)
                for k in range(ZH):
                    at = (tile * ZH + k) * PLACES
                    cut = slice(side * LANES, (side + 1) * LANES)
                    values[own, at : at + PLACES, cut] = a[k].astype(jnp.bfloat16)


def beams_kernel(spectra_ref, weight, out_ref, wide, values):
    arrange(spectra_ref, wide, values)
    for channel in range(OWN):
        here = values[channel]
        by_re = jnp.dot(weight[channel, 0], here, preferred_element_type=jnp.float32)
        by_im = jnp.dot(weight[channel, 1], here, preferred_element_type=jnp.float32)
        parts = (by_re[:, :LANES] - by_im[:, LANES:], by_re[:, LANES:] + by_im[:, :LANES])
        for side, part in enumerate(parts):
            part = pltpu.roll(part, LATE, 1) * (1.0 / math.sqrt(INPUTS))
            out_ref[side, channel] = part.astype(jnp.bfloat16)


def beams(received, weight):
    vmem = pl.BlockSpec(memory_space=pltpu.VMEM)
    return pl.pallas_call(
        beams_kernel,
        in_specs=[vmem, vmem],
        out_specs=vmem,
        out_shape=jax.ShapeDtypeStruct((2, OWN, BEAMS, FRAMES), jnp.bfloat16),
        scratch_shapes=[
            pltpu.VMEM((DEVICES * 2 * OWN, LANES), jnp.float32),
            pltpu.VMEM((OWN, INPUTS, 2 * LANES), jnp.bfloat16),
        ],
        compiler_params=pltpu.CompilerParams(vmem_limit_bytes=20 << 20),
        cost_estimate=pl.CostEstimate(
            flops=8 * OWN * BEAMS * INPUTS * FRAMES, bytes_accessed=11 << 20, transcendentals=0
        ),
    )(received, resident(weight))


def body(samples, coeffs, delays):
    first = (lax.axis_index(ALL) * OWN).astype(jnp.float32).reshape(1)
    keep = jnp.where(lax.axis_index("zh") == ZH - 1, 0.0, 1.0).astype(jnp.float32).reshape(1)
    table = jnp.asarray(dft_tables())
    up = [(i, i + 1) for i in range(ZH - 1)]
    down = [(i, (i - 1) % ZH) for i in range(ZH)]

    step = YX * ROWS
    parts = []
    for h in range(CHUNKS):
        part = samples[h * step : (h + 1) * step].reshape(YX, ROWS, 2 * FRAME)
        part, samples = lax.optimization_barrier((part, samples))
        parts.append(part)
    owns = [lax.all_to_all(part, ("y", "x"), 0, 0, tiled=True) for part in parts]
    blocks = ()
    for h, own in enumerate(owns):
        prev = lax.ppermute(own[YX - HALO :], "zh", up)
        following = lax.ppermute(own[:HALO], "zh", down)
        blocks = (spectra(h, keep, prev, own, following, coeffs, table, blocks),)

    ordered = delays.reshape(BEAMS, INP, CHUNKS, YX, ROWS).transpose(0, 2, 4, 3, 1)
    weight = weights(first, ordered.reshape(BEAMS, INPUTS))
    received = lax.all_to_all(blocks[0], ALL, 0, 0, tiled=True)
    return beams(received, weight)


def solution(mesh):
    fine = Mesh(mesh.devices.reshape(4, 4, 4, 2, 2), ALL)
    in_specs = (P(("zl", "core"), ("zh", "y", "x")), P(), P())
    out_specs = P(None, ALL, None, None)
    return jax.shard_map(body, mesh=fine, in_specs=in_specs, out_specs=out_specs, check_vma=False)
```

```python
import math

import jax
import jax.numpy as jnp
import numpy as np
from jax import lax
from jax.experimental import pallas as pl
from jax.experimental.pallas import tpu as pltpu
from jax.sharding import Mesh
from jax.sharding import PartitionSpec as P

CHAN = 1024
FRAME = 2048
TAPS = 16
INPUTS = 1024
BEAMS = 512
FRAMES = 128

ZH, YX, INP, DEVICES = 4, 16, 4, 256
PLANE = FRAMES // ZH
LATE = 8
HALO = LATE // 2
PART = PLANE // 2
ROWS = INPUTS // INP // YX
OWN = CHAN // DEVICES
PLACES = YX * INP
LANES = 128
ALL = ("zh", "y", "x", "zl", "core")


def dft_tables():
    turn = np.arange(FRAME) * (2.0 * np.pi / FRAME)
    index = np.outer(np.arange(CHAN), np.arange(FRAME // 2)) % FRAME
    table = np.stack([np.cos(turn)[index], -np.sin(turn)[index]], axis=1)
    table = table.reshape(CHAN // 2, 2, 2, FRAME // 2).transpose(1, 0, 2, 3)
    return table.reshape(2, CHAN, FRAME // 2).astype(jnp.bfloat16)


def filter_frames(frame, count, taps, turned, at, keep=None):
    frames = [frame(k) for k in range(count + TAPS - 1)]
    for j in range(count):
        newest = TAPS - 1 + j
        near = TAPS if keep is None else j + 1
        total = taps[0] * frames[newest]
        for t in range(1, near):
            total = total + taps[t] * frames[newest - t]
        if near < TAPS:
            old = taps[near] * frames[newest - near]
            for t in range(near + 1, TAPS):
                old = old + taps[t] * frames[newest - t]
            total = total + keep * old
        turned[pl.ds(at + j, ROWS, stride=PART), :] = total


def resident(value):
    return pltpu.with_memory_space_constraint(value, pltpu.VMEM)


def spectra_kernel(outer, *refs):
    if outer:
        keep_ref, prev_ref, next_ref, own_ref, coeffs_ref, table_ref, _, out_ref, *scratch = refs
    else:
        own_ref, coeffs_ref, table_ref, out_ref, *scratch = refs
    tables, sums, turned, result, table_sems, out_sems = scratch
    steps = out_sems.shape[0]
    block = CHAN // steps

    def table_copy(step):
        cut = pl.ds(step * block, block)
        return pltpu.make_async_copy(table_ref.at[:, cut], tables.at[:, cut], table_sems.at[step])

    def out_copy(step):
        cut = pl.ds(step * block // 4, block // 4)
        lanes = pl.ds(int(outer) * ROWS * PART, ROWS * PART)
        return pltpu.make_async_copy(result.at[cut], out_ref.at[cut, :, lanes], out_sems.at[step])

    for step in range(steps):
        table_copy(step).start()

    def tile(step, carry):
        for side in range(2):
            base = pl.multiple_of(step * LANES, LANES) + side * (FRAME // 2)

            def load(ref, k):
                return ref[k // 2, :, pl.ds(base + (k % 2) * FRAME, LANES)].astype(jnp.float32)

            def late(k):
                k += PLANE + LATE - (TAPS - 1 + LATE)
                return load(own_ref, k) if k < PLANE else load(next_ref, k - PLANE)

            def early(k):
                k -= TAPS - 1 - LATE
                return load(own_ref, k) if k >= 0 else load(prev_ref, k + LATE)

            taps = [coeffs_ref[t : t + 1, pl.ds(base, LANES)] for t in range(TAPS)]
            if outer:
                filter_frames(late, LATE, taps, turned.at[side], 0, keep_ref[0])
                filter_frames(early, LATE, taps, turned.at[side], LATE)
            else:
                filter_frames(lambda k: load(own_ref, k + 1), PART, taps, turned.at[side], 0)
        lanes = pl.ds(pl.multiple_of(step * LANES, LANES), LANES)
        first, second = turned[0], turned[1]
        sums[0, :, lanes] = (first + second).astype(jnp.bfloat16)
        sums[1, :, lanes] = (first - second).astype(jnp.bfloat16)
        return carry

    lax.fori_loop(0, FRAME // 2 // LANES, tile, 0)

    width = ROWS * PART
    upper = lax.broadcasted_iota(jnp.int32, (block // 8, 8, width), 1) < 4
    for step in range(steps):
        table_copy(step).wait()
        cut = slice(step * block, (step + 1) * block)
        even, odd = (
            lax.dot_general(
                tables[k, cut], sums[k], (((1,), (1,)), ((), ())), preferred_element_type=jnp.float32
            ).reshape(block // 8, 8, width)
            * (1.0 / math.sqrt(FRAME))
            for k in range(2)
        )
        one = jnp.where(upper, even, pltpu.roll(odd, 4, 1)).astype(jnp.bfloat16)
        two = jnp.where(upper, pltpu.roll(even, 4, 1), odd).astype(jnp.bfloat16)
        for k in range(block // 8):
            result[step * block // 4 + 2 * k] = one[k]
            result[step * block // 4 + 2 * k + 1] = two[k]
        out_copy(step).start()
    for step in range(steps):
        out_copy(step).wait()


def spectra(own, coeffs, table, halo=(), inner=()):
    steps = 4
    outer = len(halo) > 0
    vmem = pl.BlockSpec(memory_space=pltpu.VMEM)
    hbm = pl.BlockSpec(memory_space=pl.ANY)
    return pl.pallas_call(
        lambda *refs: spectra_kernel(outer, *refs),
        in_specs=([pl.BlockSpec(memory_space=pltpu.SMEM), vmem, vmem] if outer else [])
        + [vmem, vmem, hbm]
        + [hbm] * outer,
        out_specs=hbm,
        out_shape=jax.ShapeDtypeStruct((DEVICES, 2 * OWN, ROWS * PLANE), jnp.bfloat16),
        scratch_shapes=[
            pltpu.VMEM(table.shape, jnp.bfloat16),
            pltpu.VMEM((2, ROWS * PART, FRAME // 2), jnp.bfloat16),
            pltpu.VMEM((2, ROWS * PART, LANES), jnp.float32),
            pltpu.VMEM((DEVICES, 2 * OWN, ROWS * PART), jnp.bfloat16),
            pltpu.SemaphoreType.DMA((steps,)),
            pltpu.SemaphoreType.DMA((steps,)),
        ],
        input_output_aliases={6: 0} if outer else {},
        compiler_params=pltpu.CompilerParams(vmem_limit_bytes=20 << 20),
        cost_estimate=pl.CostEstimate(
            flops=2 * CHAN * FRAME * ROWS * PART, bytes_accessed=7 << 20, transcendentals=0
        ),
    )(*halo, own, coeffs, pltpu.with_memory_space_constraint(table, pltpu.HBM), *inner)


def fit(values):
    nodes = (np.cos(np.pi * (np.arange(64) + 0.5) / 64) + 1.0) / 8.0
    return [float(v) for v in np.polynomial.Polynomial.fit(nodes, values(np.sqrt(nodes)), 7, domain=[0, 0.25], window=[0, 0.25]).coef]


COS = fit(lambda r: np.cos(2 * np.pi * r))
SIN = fit(lambda r: np.sin(2 * np.pi * r) / r)


def cos_sin(turns):
    rest = turns - jnp.round(turns)
    square = rest * rest
    cos, sin = COS[-1], SIN[-1]
    for a, b in zip(COS[-2::-1], SIN[-2::-1]):
        cos = cos * square + a
        sin = sin * square + b
    return cos, sin * rest


def input_order():
    order = np.arange(INPUTS).reshape(INP, YX, ROWS).transpose(2, 1, 0).reshape(-1)
    return (np.arange(INPUTS)[:, None] == order).astype(jnp.bfloat16)


def weights_kernel(first_ref, delays_ref, order_ref, out_ref, delays):
    block = 128

    def reorder(step, carry):
        at = pl.ds(pl.multiple_of(step * block, block), block)
        rest = delays_ref[at]
        total = jnp.zeros_like(rest)
        for _ in range(3):
            part = rest.astype(jnp.bfloat16)
            rest = rest - part.astype(jnp.float32)
            total = total + jnp.dot(part, order_ref[...], preferred_element_type=jnp.float32)
        delays[at] = total * (1.0 / FRAME)
        return carry

    lax.fori_loop(0, BEAMS // block, reorder, 0)
    block = 16

    def rows(step, carry):
        at = pl.ds(pl.multiple_of(step * block, block), block)
        delay = delays[at]
        step_cos, step_sin = cos_sin(delay)
        cos, sin = cos_sin(delay * first_ref[0])
        for c in range(OWN):
            if c:
                cos, sin = cos * step_cos - sin * step_sin, sin * step_cos + cos * step_sin
            out_ref[c, 0, at] = cos.astype(jnp.bfloat16)
            out_ref[c, 1, at] = (-sin).astype(jnp.bfloat16)
        return carry

    lax.fori_loop(0, BEAMS // block, rows, 0)


def weights(first, delays):
    vmem = pl.BlockSpec(memory_space=pltpu.VMEM)
    return pl.pallas_call(
        weights_kernel,
        in_specs=[pl.BlockSpec(memory_space=pltpu.SMEM), vmem, vmem],
        out_specs=vmem,
        out_shape=pltpu.VMEM((OWN, 2, BEAMS, INPUTS), jnp.bfloat16),
        scratch_shapes=[pltpu.VMEM((BEAMS, INPUTS), jnp.float32)],
        compiler_params=pltpu.CompilerParams(vmem_limit_bytes=20 << 20),
        cost_estimate=pl.CostEstimate(
            flops=60 * BEAMS * INPUTS, bytes_accessed=12 << 20, transcendentals=0
        ),
    )(first, delays, jnp.asarray(input_order()))


def arrange(spectra_ref, wide, values):
    lane = lax.broadcasted_iota(jnp.int32, (PLACES, LANES), 1)
    group = LANES // PART
    rows = 2 * OWN
    for half in range(ROWS // group):
        for inner in range(2):
            at = (half if inner else half + ROWS // group) * LANES
            part = spectra_ref[:, :, at : at + LANES]
            wide[inner] = part.astype(jnp.float32).reshape(DEVICES * rows, LANES)
        for own in range(OWN):
            for side in range(2):
                row = 4 * (own % 2) + 2 * (own // 2) + side
                a = [
                    wide[inner, pl.ds(zh * PLACES * rows + row, PLACES, stride=rows), :]
                    for zh in range(ZH)
                    for inner in range(2)
                ]
                for bit in (4, 2, 1):
                    keep = lax.rem(lane, 2 * bit * PART) < bit * PART
                    for k in range(group):
                        if not k & bit:
                            x, y = a[k], a[k + bit]
                            a[k] = jnp.where(keep, x, pltpu.roll(y, bit * PART, 1))
                            a[k + bit] = jnp.where(keep, pltpu.roll(x, LANES - bit * PART, 1), y)
                for k in range(group):
                    at = (half * group + k) * PLACES
                    cut = slice(side * LANES, (side + 1) * LANES)
                    values[own, at : at + PLACES, cut] = a[k].astype(jnp.bfloat16)


def beams_kernel(spectra_ref, weight, out_ref, wide, values):
    arrange(spectra_ref, wide, values)
    lane = lax.broadcasted_iota(jnp.int32, (BEAMS, LANES), 1)
    taken_over = lax.rem(lane, PLANE) < LATE
    for channel in range(OWN):
        here = values[channel]
        by_re = jnp.dot(weight[channel, 0], here, preferred_element_type=jnp.float32)
        by_im = jnp.dot(weight[channel, 1], here, preferred_element_type=jnp.float32)
        parts = (by_re[:, :LANES] - by_im[:, LANES:], by_re[:, LANES:] + by_im[:, :LANES])
        for side, part in enumerate(parts):
            part = jnp.where(taken_over, pltpu.roll(part, PLANE, 1), part) * (1.0 / math.sqrt(INPUTS))
            out_ref[side, channel] = part.astype(jnp.bfloat16)


def beams(received, weight):
    vmem = pl.BlockSpec(memory_space=pltpu.VMEM)
    return pl.pallas_call(
        beams_kernel,
        in_specs=[vmem, vmem],
        out_specs=vmem,
        out_shape=jax.ShapeDtypeStruct((2, OWN, BEAMS, FRAMES), jnp.bfloat16),
        scratch_shapes=[
            pltpu.VMEM((2, DEVICES * 2 * OWN, LANES), jnp.float32),
            pltpu.VMEM((OWN, INPUTS, 2 * LANES), jnp.bfloat16),
        ],
        compiler_params=pltpu.CompilerParams(vmem_limit_bytes=20 << 20),
        cost_estimate=pl.CostEstimate(
            flops=8 * OWN * BEAMS * INPUTS * FRAMES, bytes_accessed=11 << 20, transcendentals=0
        ),
    )(received, resident(weight))


def body(samples, coeffs, delays):
    first = (lax.axis_index(ALL) * OWN).astype(jnp.float32).reshape(1)
    keep = jnp.where(lax.axis_index("zh") == ZH - 1, 0.0, 1.0).astype(jnp.float32).reshape(1)
    table = jnp.asarray(dft_tables())
    up = [(i, i + 1) for i in range(ZH - 1)]
    down = [(i, (i - 1) % ZH) for i in range(ZH)]

    own = lax.all_to_all(samples.reshape(YX, ROWS, 2 * FRAME), ("y", "x"), 0, 0, tiled=True)
    prev = lax.ppermute(own[YX - HALO :], "zh", up)
    following = lax.ppermute(own[:HALO], "zh", down)
    weight = weights(first, delays)
    inner = spectra(own, coeffs, table)
    prev, weight = lax.optimization_barrier((prev, weight))
    blocks = spectra(own, coeffs, table, (keep, prev, following), (inner,))
    received = lax.all_to_all(blocks, ALL, 0, 0, tiled=True)
    return beams(received, weight)


def solution(mesh):
    fine = Mesh(mesh.devices.reshape(4, 4, 4, 2, 2), ALL)
    in_specs = (P(("zl", "core"), ("zh", "y", "x")), P(), P())
    out_specs = P(None, ALL, None, None)
    return jax.shard_map(body, mesh=fine, in_specs=in_specs, out_specs=out_specs, check_vma=False)
```

```python
import math

import jax
import jax.numpy as jnp
import numpy as np
from jax import lax
from jax.experimental import pallas as pl
from jax.experimental.pallas import tpu as pltpu
from jax.sharding import Mesh
from jax.sharding import PartitionSpec as P

CHAN = 1024
FRAME = 2048
TAPS = 16
INPUTS = 1024
BEAMS = 512
FRAMES = 128

ZH, YX, INP, DEVICES = 4, 16, 4, 256
PLANE = FRAMES // ZH
LATE = 8
HALO = LATE // 2
PART = PLANE // 2
ROWS = INPUTS // INP // YX
OWN = CHAN // DEVICES
PLACES = YX * INP
LANES = 128
ALL = ("zh", "y", "x", "zl", "core")


def dft_tables():
    turn = np.arange(FRAME) * (2.0 * np.pi / FRAME)
    index = np.outer(np.arange(CHAN), np.arange(FRAME // 2)) % FRAME
    table = np.stack([np.cos(turn)[index], -np.sin(turn)[index]], axis=1)
    table = table.reshape(CHAN // 2, 2, 2, FRAME // 2).transpose(1, 0, 2, 3)
    return table.reshape(2, CHAN, FRAME // 2).astype(jnp.bfloat16)


def weighted(frame, taps, newest, delays):
    delays = list(delays)
    total = taps[delays[0]] * frame(newest - delays[0])
    for t in delays[1:]:
        total = total + taps[t] * frame(newest - t)
    return total


def resident(value):
    return pltpu.with_memory_space_constraint(value, pltpu.VMEM)


def transform(sums, tables, result, out_ref, lanes, out_sems, ready):
    steps = out_sems.shape[0]
    block = CHAN // steps
    upper = lax.broadcasted_iota(jnp.int32, (block // 8, 8, ROWS * PART), 1) < 4
    copies = []
    for step in range(steps):
        ready(step)
        cut = slice(step * block, (step + 1) * block)
        even, odd = (
            lax.dot_general(
                tables[k, cut], sums[k], (((1,), (1,)), ((), ())), preferred_element_type=jnp.float32
            ).reshape(block // 8, 8, ROWS * PART)
            * (1.0 / math.sqrt(FRAME))
            for k in range(2)
        )
        one = jnp.where(upper, even, pltpu.roll(odd, 4, 1)).astype(jnp.bfloat16)
        two = jnp.where(upper, pltpu.roll(even, 4, 1), odd).astype(jnp.bfloat16)
        for k in range(block // 8):
            result[step * block // 4 + 2 * k] = one[k]
            result[step * block // 4 + 2 * k + 1] = two[k]
        cut = pl.ds(step * block // 4, block // 4)
        copies.append(pltpu.make_async_copy(result.at[cut], out_ref.at[cut, :, lanes], out_sems.at[step]))
        copies[-1].start()
    for copy in copies:
        copy.wait()


def add_sums(sums, turned, step):
    lanes = pl.ds(pl.multiple_of(step * LANES, LANES), LANES)
    first, second = turned[0], turned[1]
    sums[0, :, lanes] = (first + second).astype(jnp.bfloat16)
    sums[1, :, lanes] = (first - second).astype(jnp.bfloat16)


def loader(ref, base):
    memo = {}

    def load(k):
        if k not in memo:
            memo[k] = ref[k // 2, :, pl.ds(base + (k % 2) * FRAME, LANES)].astype(jnp.float32)
        return memo[k]

    return load


def inner_kernel(keep_ref, own_ref, coeffs_ref, table_ref, out_ref, tables, partial_ref, *scratch):
    sums, turned, result, table_sems, out_sems = scratch
    steps = table_sems.shape[0]
    block = CHAN // steps

    def table_copy(step):
        cut = pl.ds(step * block, block)
        return pltpu.make_async_copy(table_ref.at[:, cut], tables.at[:, cut], table_sems.at[step])

    for step in range(steps):
        table_copy(step).start()

    def tile(step, carry):
        for side in range(2):
            base = pl.multiple_of(step * LANES, LANES) + side * (FRAME // 2)
            own = loader(own_ref, base)
            taps = [coeffs_ref[t : t + 1, pl.ds(base, LANES)] for t in range(TAPS)]
            for j in range(LATE):
                partial_ref[step, side, LATE + j] = weighted(own, taps, LATE + j, range(LATE + j + 1))
            for j in range(PART):
                turned[side, pl.ds(j, ROWS, stride=PART), :] = weighted(own, taps, PART + j, range(TAPS))
            for j in range(LATE):
                part = weighted(own, taps, PLANE + j, range(j + 1, TAPS))
                partial_ref[step, side, j] = part * keep_ref[0]
        add_sums(sums, turned, step)
        return carry

    lax.fori_loop(0, FRAME // 2 // LANES, tile, 0)
    lanes = pl.ds(0, ROWS * PART)
    transform(sums, tables, result, out_ref, lanes, out_sems, lambda step: table_copy(step).wait())


def outer_kernel(prev_ref, next_ref, coeffs_ref, tables, partial_ref, _, out_ref, *scratch):
    sums, turned, result, out_sems = scratch

    def tile(step, carry):
        for side in range(2):
            base = pl.multiple_of(step * LANES, LANES) + side * (FRAME // 2)
            prev, following = loader(prev_ref, base), loader(next_ref, base)
            taps = [coeffs_ref[t : t + 1, pl.ds(base, LANES)] for t in range(TAPS)]
            for j in range(LATE):
                total = partial_ref[step, side, j] + weighted(following, taps, j, range(j + 1))
                turned[side, pl.ds(j, ROWS, stride=PART), :] = total
                total = partial_ref[step, side, LATE + j]
                if LATE + j + 1 < TAPS:
                    total = total + weighted(prev, taps, 2 * LATE + j, range(LATE + j + 1, TAPS))
                turned[side, pl.ds(LATE + j, ROWS, stride=PART), :] = total
        add_sums(sums, turned, step)
        return carry

    lax.fori_loop(0, FRAME // 2 // LANES, tile, 0)
    lanes = pl.ds(ROWS * PART, ROWS * PART)
    transform(sums, tables, result, out_ref, lanes, out_sems, lambda step: None)


SPECTRA = jax.ShapeDtypeStruct((DEVICES, 2 * OWN, ROWS * PLANE), jnp.bfloat16)
STEPS = 4
SPECTRA_SCRATCH = [
    pltpu.VMEM((2, ROWS * PART, FRAME // 2), jnp.bfloat16),
    pltpu.VMEM((2, ROWS * PART, LANES), jnp.float32),
    pltpu.VMEM((DEVICES, 2 * OWN, ROWS * PART), jnp.bfloat16),
]
SEMS = pltpu.SemaphoreType.DMA((STEPS,))


def inner_spectra(keep, own, coeffs, table):
    smem, vmem, hbm = (pl.BlockSpec(memory_space=m) for m in (pltpu.SMEM, pltpu.VMEM, pl.ANY))
    partial = (FRAME // 2 // LANES, 2, PART, ROWS, LANES)
    return pl.pallas_call(
        inner_kernel,
        in_specs=[smem, vmem, vmem, hbm],
        out_specs=[hbm, vmem, vmem],
        out_shape=[SPECTRA, pltpu.VMEM(table.shape, table.dtype), pltpu.VMEM(partial, jnp.float32)],
        scratch_shapes=SPECTRA_SCRATCH + [SEMS, SEMS],
        compiler_params=pltpu.CompilerParams(vmem_limit_bytes=20 << 20),
        cost_estimate=pl.CostEstimate(
            flops=2 * CHAN * FRAME * ROWS * PART, bytes_accessed=7 << 20, transcendentals=0
        ),
    )(keep, own, coeffs, pltpu.with_memory_space_constraint(table, pltpu.HBM))


def outer_spectra(prev, following, coeffs, tables, partial, inner):
    vmem, hbm = (pl.BlockSpec(memory_space=m) for m in (pltpu.VMEM, pl.ANY))
    return pl.pallas_call(
        outer_kernel,
        in_specs=[vmem] * 5 + [hbm],
        out_specs=hbm,
        out_shape=SPECTRA,
        scratch_shapes=SPECTRA_SCRATCH + [SEMS],
        input_output_aliases={5: 0},
        compiler_params=pltpu.CompilerParams(vmem_limit_bytes=16 << 20),
        cost_estimate=pl.CostEstimate(
            flops=2 * CHAN * FRAME * ROWS * PART, bytes_accessed=7 << 20, transcendentals=0
        ),
    )(prev, following, coeffs, resident(tables), resident(partial), inner)


def fit(values):
    nodes = (np.cos(np.pi * (np.arange(64) + 0.5) / 64) + 1.0) / 8.0
    return [float(v) for v in np.polynomial.Polynomial.fit(nodes, values(np.sqrt(nodes)), 6, domain=[0, 0.25], window=[0, 0.25]).coef]


COS = fit(lambda r: np.cos(2 * np.pi * r))
SIN = fit(lambda r: np.sin(2 * np.pi * r) / r)


def cos_sin(turns):
    rest = turns - jnp.round(turns)
    square = rest * rest
    cos, sin = COS[-1], SIN[-1]
    for a, b in zip(COS[-2::-1], SIN[-2::-1]):
        cos = cos * square + a
        sin = sin * square + b
    return cos, sin * rest


def input_order():
    order = np.arange(INPUTS).reshape(INP, YX, ROWS).transpose(2, 1, 0).reshape(-1)
    return (np.arange(INPUTS)[:, None] == order).astype(jnp.bfloat16)


def weights_kernel(first_ref, delays_hbm, order_hbm, out_ref, delays, delays_ref, order_ref, sems):
    copies = [
        pltpu.make_async_copy(delays_hbm, delays_ref, sems.at[0]),
        pltpu.make_async_copy(order_hbm, order_ref, sems.at[1]),
    ]
    for copy in copies:
        copy.start()
    for copy in copies:
        copy.wait()
    block = 128

    def reorder(step, carry):
        at = pl.ds(pl.multiple_of(step * block, block), block)
        rest = delays_ref[at]
        total = jnp.zeros_like(rest)
        for _ in range(3):
            part = rest.astype(jnp.bfloat16)
            rest = rest - part.astype(jnp.float32)
            total = total + jnp.dot(part, order_ref[...], preferred_element_type=jnp.float32)
        delays[at] = total * (1.0 / FRAME)
        return carry

    lax.fori_loop(0, BEAMS // block, reorder, 0)
    block = 16

    def rows(step, carry):
        at = pl.ds(pl.multiple_of(step * block, block), block)
        delay = delays[at]
        step_cos, step_sin = cos_sin(delay)
        cos, sin = cos_sin(delay * first_ref[0])
        for c in range(OWN):
            if c:
                cos, sin = cos * step_cos - sin * step_sin, sin * step_cos + cos * step_sin
            out_ref[c, 0, at] = cos.astype(jnp.bfloat16)
            out_ref[c, 1, at] = (-sin).astype(jnp.bfloat16)
        return carry

    lax.fori_loop(0, BEAMS // block, rows, 0)


def weights(first, delays):
    vmem = pl.BlockSpec(memory_space=pltpu.VMEM)
    return pl.pallas_call(
        weights_kernel,
        in_specs=[pl.BlockSpec(memory_space=m) for m in (pltpu.SMEM, pl.ANY, pl.ANY)],
        out_specs=vmem,
        out_shape=pltpu.VMEM((OWN, 2, BEAMS, INPUTS), jnp.bfloat16),
        scratch_shapes=[
            pltpu.VMEM((BEAMS, INPUTS), jnp.float32),
            pltpu.VMEM((BEAMS, INPUTS), jnp.float32),
            pltpu.VMEM((INPUTS, INPUTS), jnp.bfloat16),
            pltpu.SemaphoreType.DMA((2,)),
        ],
        compiler_params=pltpu.CompilerParams(vmem_limit_bytes=20 << 20),
        cost_estimate=pl.CostEstimate(
            flops=60 * BEAMS * INPUTS, bytes_accessed=12 << 20, transcendentals=0
        ),
    )(
        first,
        pltpu.with_memory_space_constraint(delays, pltpu.HBM),
        pltpu.with_memory_space_constraint(jnp.asarray(input_order()), pltpu.HBM),
    )


def arrange(wide, own, values):
    lane = lax.broadcasted_iota(jnp.int32, (PLACES, LANES), 1)
    group = LANES // PART
    rows = 2 * OWN
    halves = ROWS // group
    for half in range(halves):
        for side in range(2):
            row = 4 * (own % 2) + 2 * (own // 2) + side
            a = [
                wide[half + (1 - inner) * halves, pl.ds(zh * PLACES * rows + row, PLACES, stride=rows), :]
                for zh in range(ZH)
                for inner in range(2)
            ]
            for bit in (4, 2, 1):
                keep = lax.rem(lane, 2 * bit * PART) < bit * PART
                for k in range(group):
                    if not k & bit:
                        x, y = a[k], a[k + bit]
                        a[k] = jnp.where(keep, x, pltpu.roll(y, bit * PART, 1))
                        a[k + bit] = jnp.where(keep, pltpu.roll(x, LANES - bit * PART, 1), y)
            for k in range(group):
                at = (half * group + k) * PLACES
                values[at : at + PLACES, side * LANES : (side + 1) * LANES] = a[k].astype(jnp.bfloat16)


def beams_kernel(spectra_ref, weight, out_ref, wide, values, result, sems):
    for tile in range(ROWS * PLANE // LANES):
        part = spectra_ref[:, :, tile * LANES : (tile + 1) * LANES]
        wide[tile] = part.astype(jnp.float32).reshape(DEVICES * 2 * OWN, LANES)
    lane = lax.broadcasted_iota(jnp.int32, (BEAMS, LANES), 1)
    taken_over = lax.rem(lane, PLANE) < LATE
    copies = []
    for channel in range(OWN):
        arrange(wide, channel, values.at[channel])
        here = values[channel]
        by_re = jnp.dot(weight[channel, 0], here, preferred_element_type=jnp.float32)
        by_im = jnp.dot(weight[channel, 1], here, preferred_element_type=jnp.float32)
        parts = (by_re[:, :LANES] - by_im[:, LANES:], by_re[:, LANES:] + by_im[:, :LANES])
        for side, part in enumerate(parts):
            part = jnp.where(taken_over, pltpu.roll(part, PLANE, 1), part) * (1.0 / math.sqrt(INPUTS))
            result[side, channel] = part.astype(jnp.bfloat16)
        copies.append(pltpu.make_async_copy(result.at[:, channel], out_ref.at[:, channel], sems.at[channel]))
        copies[-1].start()
    for copy in copies:
        copy.wait()


def beams(received, weight):
    vmem = pl.BlockSpec(memory_space=pltpu.VMEM)
    shape = (2, OWN, BEAMS, FRAMES)
    return pl.pallas_call(
        beams_kernel,
        in_specs=[vmem, vmem],
        out_specs=pl.BlockSpec(memory_space=pl.ANY),
        out_shape=jax.ShapeDtypeStruct(shape, jnp.bfloat16),
        scratch_shapes=[
            pltpu.VMEM((ROWS * PLANE // LANES, DEVICES * 2 * OWN, LANES), jnp.float32),
            pltpu.VMEM((OWN, INPUTS, 2 * LANES), jnp.bfloat16),
            pltpu.VMEM(shape, jnp.bfloat16),
            pltpu.SemaphoreType.DMA((OWN,)),
        ],
        compiler_params=pltpu.CompilerParams(vmem_limit_bytes=20 << 20),
        cost_estimate=pl.CostEstimate(
            flops=8 * OWN * BEAMS * INPUTS * FRAMES, bytes_accessed=11 << 20, transcendentals=0
        ),
    )(received, resident(weight))


def body(samples, coeffs, delays):
    first = (lax.axis_index(ALL) * OWN).astype(jnp.float32).reshape(1)
    keep = jnp.where(lax.axis_index("zh") == ZH - 1, 0.0, 1.0).astype(jnp.float32).reshape(1)
    table = jnp.asarray(dft_tables())
    up = [(i, i + 1) for i in range(ZH - 1)]
    down = [(i, (i - 1) % ZH) for i in range(ZH)]

    own = lax.all_to_all(samples.reshape(YX, ROWS, 2 * FRAME), ("y", "x"), 0, 0, tiled=True)
    prev = lax.ppermute(own[YX - HALO :], "zh", up)
    following = lax.ppermute(own[:HALO], "zh", down)
    weight = weights(first, delays)
    inner, tables, partial = inner_spectra(keep, own, coeffs, table)
    prev, weight = lax.optimization_barrier((prev, weight))
    blocks = outer_spectra(prev, following, coeffs, tables, partial, inner)
    received = lax.all_to_all(blocks, ALL, 0, 0, tiled=True)
    return beams(received, weight)


def solution(mesh):
    fine = Mesh(mesh.devices.reshape(4, 4, 4, 2, 2), ALL)
    in_specs = (P(("zl", "core"), ("zh", "y", "x")), P(), P())
    out_specs = P(None, ALL, None, None)
    return jax.shard_map(body, mesh=fine, in_specs=in_specs, out_specs=out_specs, check_vma=False)
```

```python
import math

import jax
import jax.numpy as jnp
import numpy as np
from jax import lax
from jax.experimental import pallas as pl
from jax.experimental.pallas import tpu as pltpu
from jax.sharding import Mesh
from jax.sharding import PartitionSpec as P

CHAN = 1024
FRAME = 2048
TAPS = 16
INPUTS = 1024
BEAMS = 512
FRAMES = 128

ZH, YX, INP, DEVICES = 4, 16, 4, 256
PLANE = FRAMES // ZH
LATE = 8
HALO = LATE // 2
PART = PLANE // 2
ROWS = INPUTS // INP // YX
OWN = CHAN // DEVICES
PLACES = YX * INP
LANES = 128
GROUP = LANES // PART
ALL = ("zh", "y", "x", "zl", "core")


def dft_tables():
    turn = np.arange(FRAME) * (2.0 * np.pi / FRAME)
    index = np.outer(np.arange(CHAN), np.arange(FRAME // 2)) % FRAME
    table = np.stack([np.cos(turn)[index], -np.sin(turn)[index]], axis=1)
    table = table.reshape(CHAN // 2, 2, 2, FRAME // 2).transpose(1, 0, 2, 3)
    return table.reshape(2, CHAN, FRAME // 2).astype(jnp.bfloat16)


def weighted(frame, taps, newest, delays):
    delays = list(delays)
    total = taps[delays[0]] * frame(newest - delays[0])
    for t in delays[1:]:
        total = total + taps[t] * frame(newest - t)
    return total


def resident(value):
    return pltpu.with_memory_space_constraint(value, pltpu.VMEM)


def transform(sums, tables, result, out_ref, lanes, out_sems, ready):
    steps = out_sems.shape[0]
    block = CHAN // steps
    upper = lax.broadcasted_iota(jnp.int32, (block // 8, 8, ROWS * PART), 1) < 4
    copies = []
    for step in range(steps):
        ready(step)
        cut = slice(step * block, (step + 1) * block)
        even, odd = (
            lax.dot_general(
                tables[k, cut], sums[k], (((1,), (1,)), ((), ())), preferred_element_type=jnp.float32
            ).reshape(block // 8, 8, ROWS * PART)
            * (1.0 / math.sqrt(FRAME))
            for k in range(2)
        )
        one = jnp.where(upper, even, pltpu.roll(odd, 4, 1)).astype(jnp.bfloat16)
        two = jnp.where(upper, pltpu.roll(even, 4, 1), odd).astype(jnp.bfloat16)
        for k in range(block // 8):
            result[step * block // 4 + 2 * k] = one[k]
            result[step * block // 4 + 2 * k + 1] = two[k]
        cut = pl.ds(step * block // 4, block // 4)
        copies.append(pltpu.make_async_copy(result.at[cut], out_ref.at[cut, :, lanes], out_sems.at[step]))
        copies[-1].start()
    for copy in copies:
        copy.wait()


def add_sums(sums, turned, step, shift):
    lanes = pl.ds(pl.multiple_of(step * LANES, LANES), LANES)
    for k in range(ROWS):
        first, second = (turned[side, k * PART : (k + 1) * PART] for side in range(2))
        to = k // GROUP * GROUP + lax.rem(k % GROUP + shift, GROUP)
        to = pl.ds(pl.multiple_of(to * PART, PART), PART)
        sums[0, to, lanes] = (first + second).astype(jnp.bfloat16)
        sums[1, to, lanes] = (first - second).astype(jnp.bfloat16)


def loader(ref, base):
    memo = {}

    def load(k):
        if k not in memo:
            memo[k] = ref[k // 2, :, pl.ds(base + (k % 2) * FRAME, LANES)].astype(jnp.float32)
        return memo[k]

    return load


def inner_kernel(zh_ref, own_ref, coeffs_ref, table_ref, out_ref, tables, partial_ref, *scratch):
    sums, turned, result, table_sems, out_sems = scratch
    steps = table_sems.shape[0]
    block = CHAN // steps
    keep = jnp.where(zh_ref[0] == ZH - 1, 0.0, 1.0)

    def table_copy(step):
        cut = pl.ds(step * block, block)
        return pltpu.make_async_copy(table_ref.at[:, cut], tables.at[:, cut], table_sems.at[step])

    for step in range(steps):
        table_copy(step).start()

    def tile(step, carry):
        for side in range(2):
            base = pl.multiple_of(step * LANES, LANES) + side * (FRAME // 2)
            own = loader(own_ref, base)
            taps = [coeffs_ref[t : t + 1, pl.ds(base, LANES)] for t in range(TAPS)]
            for j in range(LATE):
                partial_ref[step, side, LATE + j] = weighted(own, taps, LATE + j, range(LATE + j + 1))
            for j in range(PART):
                turned[side, pl.ds(j, ROWS, stride=PART), :] = weighted(own, taps, PART + j, range(TAPS))
            for j in range(LATE):
                part = weighted(own, taps, PLANE + j, range(j + 1, TAPS))
                partial_ref[step, side, j] = part * keep
        add_sums(sums, turned, step, 2 * zh_ref[0] + 1)
        return carry

    lax.fori_loop(0, FRAME // 2 // LANES, tile, 0)
    lanes = pl.ds(0, ROWS * PART)
    transform(sums, tables, result, out_ref, lanes, out_sems, lambda step: table_copy(step).wait())


def outer_kernel(zh_ref, prev_ref, next_ref, coeffs_ref, tables, partial_ref, _, out_ref, *scratch):
    sums, turned, result, out_sems = scratch

    def tile(step, carry):
        for side in range(2):
            base = pl.multiple_of(step * LANES, LANES) + side * (FRAME // 2)
            prev, following = loader(prev_ref, base), loader(next_ref, base)
            taps = [coeffs_ref[t : t + 1, pl.ds(base, LANES)] for t in range(TAPS)]
            for j in range(LATE):
                total = partial_ref[step, side, j] + weighted(following, taps, j, range(j + 1))
                turned[side, pl.ds(j, ROWS, stride=PART), :] = total
                total = partial_ref[step, side, LATE + j]
                if LATE + j + 1 < TAPS:
                    total = total + weighted(prev, taps, 2 * LATE + j, range(LATE + j + 1, TAPS))
                turned[side, pl.ds(LATE + j, ROWS, stride=PART), :] = total
        add_sums(sums, turned, step, 2 * zh_ref[0])
        return carry

    lax.fori_loop(0, FRAME // 2 // LANES, tile, 0)
    lanes = pl.ds(ROWS * PART, ROWS * PART)
    transform(sums, tables, result, out_ref, lanes, out_sems, lambda step: None)


SPECTRA = jax.ShapeDtypeStruct((DEVICES, 2 * OWN, ROWS * PLANE), jnp.bfloat16)
STEPS = 4
SPECTRA_SCRATCH = [
    pltpu.VMEM((2, ROWS * PART, FRAME // 2), jnp.bfloat16),
    pltpu.VMEM((2, ROWS * PART, LANES), jnp.float32),
    pltpu.VMEM((DEVICES, 2 * OWN, ROWS * PART), jnp.bfloat16),
]
SEMS = pltpu.SemaphoreType.DMA((STEPS,))


def inner_spectra(zh, own, coeffs, table):
    smem, vmem, hbm = (pl.BlockSpec(memory_space=m) for m in (pltpu.SMEM, pltpu.VMEM, pl.ANY))
    partial = (FRAME // 2 // LANES, 2, PART, ROWS, LANES)
    return pl.pallas_call(
        inner_kernel,
        in_specs=[smem, vmem, vmem, hbm],
        out_specs=[hbm, vmem, vmem],
        out_shape=[SPECTRA, pltpu.VMEM(table.shape, table.dtype), pltpu.VMEM(partial, jnp.float32)],
        scratch_shapes=SPECTRA_SCRATCH + [SEMS, SEMS],
        compiler_params=pltpu.CompilerParams(vmem_limit_bytes=20 << 20),
        cost_estimate=pl.CostEstimate(
            flops=2 * CHAN * FRAME * ROWS * PART, bytes_accessed=7 << 20, transcendentals=0
        ),
    )(zh, own, coeffs, pltpu.with_memory_space_constraint(table, pltpu.HBM))


def outer_spectra(zh, prev, following, coeffs, tables, partial, inner):
    smem, vmem, hbm = (pl.BlockSpec(memory_space=m) for m in (pltpu.SMEM, pltpu.VMEM, pl.ANY))
    return pl.pallas_call(
        outer_kernel,
        in_specs=[smem] + [vmem] * 5 + [hbm],
        out_specs=hbm,
        out_shape=SPECTRA,
        scratch_shapes=SPECTRA_SCRATCH + [SEMS],
        input_output_aliases={6: 0},
        compiler_params=pltpu.CompilerParams(vmem_limit_bytes=16 << 20),
        cost_estimate=pl.CostEstimate(
            flops=2 * CHAN * FRAME * ROWS * PART, bytes_accessed=7 << 20, transcendentals=0
        ),
    )(zh, prev, following, coeffs, resident(tables), resident(partial), inner)


def fit(values):
    nodes = (np.cos(np.pi * (np.arange(64) + 0.5) / 64) + 1.0) / 8.0
    return [float(v) for v in np.polynomial.Polynomial.fit(nodes, values(np.sqrt(nodes)), 6, domain=[0, 0.25], window=[0, 0.25]).coef]


COS = fit(lambda r: np.cos(2 * np.pi * r))
SIN = fit(lambda r: np.sin(2 * np.pi * r) / r)


def cos_sin(turns):
    rest = turns - jnp.round(turns)
    square = rest * rest
    cos, sin = COS[-1], SIN[-1]
    for a, b in zip(COS[-2::-1], SIN[-2::-1]):
        cos = cos * square + a
        sin = sin * square + b
    return cos, sin * rest


def input_order():
    order = np.arange(INPUTS).reshape(INP, YX, ROWS).transpose(2, 1, 0).reshape(-1)
    return (np.arange(INPUTS)[:, None] == order).astype(jnp.bfloat16)


def weights_kernel(first_ref, delays_hbm, order_hbm, out_ref, delays, delays_ref, order_ref, sems):
    copies = [
        pltpu.make_async_copy(delays_hbm, delays_ref, sems.at[0]),
        pltpu.make_async_copy(order_hbm, order_ref, sems.at[1]),
    ]
    for copy in copies:
        copy.start()
    for copy in copies:
        copy.wait()
    block = 128

    def reorder(step, carry):
        at = pl.ds(pl.multiple_of(step * block, block), block)
        rest = delays_ref[at]
        total = jnp.zeros_like(rest)
        for _ in range(3):
            part = rest.astype(jnp.bfloat16)
            rest = rest - part.astype(jnp.float32)
            total = total + jnp.dot(part, order_ref[...], preferred_element_type=jnp.float32)
        delays[at] = total * (1.0 / FRAME)
        return carry

    lax.fori_loop(0, BEAMS // block, reorder, 0)
    block = 16

    def rows(step, carry):
        at = pl.ds(pl.multiple_of(step * block, block), block)
        delay = delays[at]
        step_cos, step_sin = cos_sin(delay)
        cos, sin = cos_sin(delay * first_ref[0])
        for c in range(OWN):
            if c:
                cos, sin = cos * step_cos - sin * step_sin, sin * step_cos + cos * step_sin
            out_ref[c, 0, at] = cos.astype(jnp.bfloat16)
            out_ref[c, 1, at] = (-sin).astype(jnp.bfloat16)
        return carry

    lax.fori_loop(0, BEAMS // block, rows, 0)


def weights(first, delays):
    vmem = pl.BlockSpec(memory_space=pltpu.VMEM)
    return pl.pallas_call(
        weights_kernel,
        in_specs=[pl.BlockSpec(memory_space=m) for m in (pltpu.SMEM, pl.ANY, pl.ANY)],
        out_specs=vmem,
        out_shape=pltpu.VMEM((OWN, 2, BEAMS, INPUTS), jnp.bfloat16),
        scratch_shapes=[
            pltpu.VMEM((BEAMS, INPUTS), jnp.float32),
            pltpu.VMEM((BEAMS, INPUTS), jnp.float32),
            pltpu.VMEM((INPUTS, INPUTS), jnp.bfloat16),
            pltpu.SemaphoreType.DMA((2,)),
        ],
        compiler_params=pltpu.CompilerParams(vmem_limit_bytes=20 << 20),
        cost_estimate=pl.CostEstimate(
            flops=60 * BEAMS * INPUTS, bytes_accessed=12 << 20, transcendentals=0
        ),
    )(
        first,
        pltpu.with_memory_space_constraint(delays, pltpu.HBM),
        pltpu.with_memory_space_constraint(jnp.asarray(input_order()), pltpu.HBM),
    )


def arrange(wide, own, values):
    place = lax.broadcasted_iota(jnp.int32, (PLACES, LANES), 1) // PART
    rows = 2 * OWN
    halves = ROWS // GROUP
    for half in range(halves):
        for side in range(2):
            row = 4 * (own % 2) + 2 * (own // 2) + side
            a = [
                wide[half + (1 - inner) * halves, pl.ds(zh * PLACES * rows + row, PLACES, stride=rows), :].astype(
                    jnp.bfloat16
                )
                for zh in range(ZH)
                for inner in range(2)
            ]
            for bit in (1, 2, 4):
                moved = place & bit != 0
                a = [jnp.where(moved, a[(k + bit) % GROUP], a[k]) for k in range(GROUP)]
            for k in range(GROUP):
                at = (half * GROUP + k) * PLACES
                value = a[-k % GROUP]
                value = pltpu.roll(value, LANES - k * PART, 1) if k else value
                values[at : at + PLACES, side * LANES : (side + 1) * LANES] = value


def beams_kernel(spectra_ref, weight, out_ref, wide, values, result, sems):
    for tile in range(ROWS * PLANE // LANES):
        part = spectra_ref[:, :, tile * LANES : (tile + 1) * LANES]
        wide[tile] = part.astype(jnp.float32).reshape(DEVICES * 2 * OWN, LANES)
    lane = lax.broadcasted_iota(jnp.int32, (BEAMS, LANES), 1)
    taken_over = lax.rem(lane, PLANE) < LATE
    copies = []
    for channel in range(OWN):
        arrange(wide, channel, values.at[channel])
        here = values[channel]
        by_re = jnp.dot(weight[channel, 0], here, preferred_element_type=jnp.float32)
        by_im = jnp.dot(weight[channel, 1], here, preferred_element_type=jnp.float32)
        parts = (by_re[:, :LANES] - by_im[:, LANES:], by_re[:, LANES:] + by_im[:, :LANES])
        for side, part in enumerate(parts):
            part = jnp.where(taken_over, pltpu.roll(part, PLANE, 1), part) * (1.0 / math.sqrt(INPUTS))
            result[side, channel] = part.astype(jnp.bfloat16)
        copies.append(pltpu.make_async_copy(result.at[:, channel], out_ref.at[:, channel], sems.at[channel]))
        copies[-1].start()
    for copy in copies:
        copy.wait()


def beams(received, weight):
    vmem = pl.BlockSpec(memory_space=pltpu.VMEM)
    shape = (2, OWN, BEAMS, FRAMES)
    return pl.pallas_call(
        beams_kernel,
        in_specs=[vmem, vmem],
        out_specs=pl.BlockSpec(memory_space=pl.ANY),
        out_shape=jax.ShapeDtypeStruct(shape, jnp.bfloat16),
        scratch_shapes=[
            pltpu.VMEM((ROWS * PLANE // LANES, DEVICES * 2 * OWN, LANES), jnp.float32),
            pltpu.VMEM((OWN, INPUTS, 2 * LANES), jnp.bfloat16),
            pltpu.VMEM(shape, jnp.bfloat16),
            pltpu.SemaphoreType.DMA((OWN,)),
        ],
        compiler_params=pltpu.CompilerParams(vmem_limit_bytes=20 << 20),
        cost_estimate=pl.CostEstimate(
            flops=8 * OWN * BEAMS * INPUTS * FRAMES, bytes_accessed=11 << 20, transcendentals=0
        ),
    )(received, resident(weight))


def body(samples, coeffs, delays):
    first = (lax.axis_index(ALL) * OWN).astype(jnp.float32).reshape(1)
    zh = lax.axis_index("zh").astype(jnp.int32).reshape(1)
    table = jnp.asarray(dft_tables())
    up = [(i, i + 1) for i in range(ZH - 1)]
    down = [(i, (i - 1) % ZH) for i in range(ZH)]

    own = lax.all_to_all(samples.reshape(YX, ROWS, 2 * FRAME), ("y", "x"), 0, 0, tiled=True)
    prev = lax.ppermute(own[YX - HALO :], "zh", up)
    following = lax.ppermute(own[:HALO], "zh", down)
    weight = weights(first, delays)
    inner, tables, partial = inner_spectra(zh, own, coeffs, table)
    prev, weight = lax.optimization_barrier((prev, weight))
    blocks = outer_spectra(zh, prev, following, coeffs, tables, partial, inner)
    received = lax.all_to_all(blocks, ALL, 0, 0, tiled=True)
    return beams(received, weight)


def solution(mesh):
    fine = Mesh(mesh.devices.reshape(4, 4, 4, 2, 2), ALL)
    in_specs = (P(("zl", "core"), ("zh", "y", "x")), P(), P())
    out_specs = P(None, ALL, None, None)
    return jax.shard_map(body, mesh=fine, in_specs=in_specs, out_specs=out_specs, check_vma=False)
```

```python
import math

import jax
import jax.numpy as jnp
import numpy as np
from jax import lax
from jax.experimental import pallas as pl
from jax.experimental.pallas import tpu as pltpu
from jax.sharding import Mesh
from jax.sharding import PartitionSpec as P

CHAN = 1024
FRAME = 2048
TAPS = 16
INPUTS = 1024
BEAMS = 512
FRAMES = 128

ZH, YX, INP, DEVICES = 4, 16, 4, 256
PLANE = FRAMES // ZH
LATE = 8
HALO = LATE // 2
PART = PLANE // 2
ROWS = INPUTS // INP // YX
OWN = CHAN // DEVICES
PLACES = YX * INP
LANES = 128
GROUP = LANES // PART
ALL = ("zh", "y", "x", "zl", "core")
OWNERS = ("zh", "zl", "core", "y", "x")


def dft_tables():
    turn = np.arange(FRAME) * (2.0 * np.pi / FRAME)
    index = np.outer(np.arange(CHAN), np.arange(FRAME // 2)) % FRAME
    table = np.stack([np.cos(turn)[index], -np.sin(turn)[index]], axis=1)
    table = table.reshape(ZH, YX, INP, OWN // 2, 2, 2, FRAME // 2).transpose(4, 0, 2, 1, 3, 5, 6)
    return table.reshape(2, CHAN, FRAME // 2).astype(jnp.bfloat16)


def weighted(frame, taps, newest, delays):
    delays = list(delays)
    total = taps[delays[0]] * frame(newest - delays[0])
    for t in delays[1:]:
        total = total + taps[t] * frame(newest - t)
    return total


def resident(value):
    return pltpu.with_memory_space_constraint(value, pltpu.VMEM)


def transform(sums, tables, result, out_ref, lanes, out_sems, ready):
    steps = out_sems.shape[0]
    block = CHAN // steps
    upper = lax.broadcasted_iota(jnp.int32, (block // 8, 8, ROWS * PART), 1) < 4
    copies = []
    for step in range(steps):
        ready(step)
        cut = slice(step * block, (step + 1) * block)
        even, odd = (
            lax.dot_general(
                tables[k, cut], sums[k], (((1,), (1,)), ((), ())), preferred_element_type=jnp.float32
            ).reshape(block // 8, 8, ROWS * PART)
            * (1.0 / math.sqrt(FRAME))
            for k in range(2)
        )
        one = jnp.where(upper, even, pltpu.roll(odd, 4, 1)).astype(jnp.bfloat16)
        two = jnp.where(upper, pltpu.roll(even, 4, 1), odd).astype(jnp.bfloat16)
        for k in range(block // 8):
            result[step * block // 4 + 2 * k] = one[k]
            result[step * block // 4 + 2 * k + 1] = two[k]
        cut = pl.ds(step * block // 4, block // 4)
        copies.append(pltpu.make_async_copy(result.at[cut], out_ref.at[cut, :, lanes], out_sems.at[step]))
        copies[-1].start()
    for copy in copies:
        copy.wait()


def add_sums(sums, turned, step, shift):
    lanes = pl.ds(pl.multiple_of(step * LANES, LANES), LANES)
    for k in range(ROWS):
        first, second = (turned[side, k * PART : (k + 1) * PART] for side in range(2))
        to = k // GROUP * GROUP + lax.rem(k % GROUP + shift, GROUP)
        to = pl.ds(pl.multiple_of(to * PART, PART), PART)
        sums[0, to, lanes] = (first + second).astype(jnp.bfloat16)
        sums[1, to, lanes] = (first - second).astype(jnp.bfloat16)


def loader(ref, base):
    memo = {}

    def load(k):
        if k not in memo:
            memo[k] = ref[k // 2, :, pl.ds(base + (k % 2) * FRAME, LANES)].astype(jnp.float32)
        return memo[k]

    return load


def frame_loader(ref, base):
    memo = {}

    def load(k):
        if k not in memo:
            memo[k] = ref[k, :, pl.ds(base, LANES)].astype(jnp.float32)
        return memo[k]

    return load


def inner_kernel(zh_ref, own_ref, coeffs_ref, table_ref, out_ref, tables, partial_ref, *scratch):
    sums, turned, result, table_sems, out_sems = scratch
    steps = table_sems.shape[0]
    block = CHAN // steps
    keep = jnp.where(zh_ref[0] == ZH - 1, 0.0, 1.0)

    def table_copy(step):
        cut = pl.ds(step * block, block)
        return pltpu.make_async_copy(table_ref.at[:, cut], tables.at[:, cut], table_sems.at[step])

    for step in range(steps):
        table_copy(step).start()

    def tile(step, carry):
        for side in range(2):
            base = pl.multiple_of(step * LANES, LANES) + side * (FRAME // 2)
            own = loader(own_ref, base)
            taps = [coeffs_ref[t : t + 1, pl.ds(base, LANES)] for t in range(TAPS)]
            for j in range(LATE):
                partial_ref[step, side, LATE + j] = weighted(own, taps, LATE + j, range(LATE + j + 1))
            for j in range(PART):
                turned[side, pl.ds(j, ROWS, stride=PART), :] = weighted(own, taps, PART + j, range(TAPS))
            for j in range(LATE):
                part = weighted(own, taps, PLANE + j, range(j + 1, TAPS))
                partial_ref[step, side, j] = part * keep
        add_sums(sums, turned, step, 2 * zh_ref[0] + 1)
        return carry

    lax.fori_loop(0, FRAME // 2 // LANES, tile, 0)
    lanes = pl.ds(0, ROWS * PART)
    transform(sums, tables, result, out_ref, lanes, out_sems, lambda step: table_copy(step).wait())


def outer_kernel(zh_ref, next_ref, prev_ref, coeffs_ref, tables, partial_ref, _, out_ref, *scratch):
    sums, turned, result, out_sems = scratch

    def tile(step, carry):
        for side in range(2):
            base = pl.multiple_of(step * LANES, LANES) + side * (FRAME // 2)
            prev, following = frame_loader(prev_ref, base), loader(next_ref, base)
            taps = [coeffs_ref[t : t + 1, pl.ds(base, LANES)] for t in range(TAPS)]
            for j in range(LATE):
                total = partial_ref[step, side, j] + weighted(following, taps, j, range(j + 1))
                turned[side, pl.ds(j, ROWS, stride=PART), :] = total
                total = partial_ref[step, side, LATE + j]
                if LATE + j + 1 < TAPS:
                    total = total + weighted(prev, taps, 2 * LATE - 1 + j, range(LATE + j + 1, TAPS))
                turned[side, pl.ds(LATE + j, ROWS, stride=PART), :] = total
        add_sums(sums, turned, step, 2 * zh_ref[0])
        return carry

    lax.fori_loop(0, FRAME // 2 // LANES, tile, 0)
    lanes = pl.ds(ROWS * PART, ROWS * PART)
    transform(sums, tables, result, out_ref, lanes, out_sems, lambda step: None)


SPECTRA = jax.ShapeDtypeStruct((DEVICES, 2 * OWN, ROWS * PLANE), jnp.bfloat16)
STEPS = 4
SPECTRA_SCRATCH = [
    pltpu.VMEM((2, ROWS * PART, FRAME // 2), jnp.bfloat16),
    pltpu.VMEM((2, ROWS * PART, LANES), jnp.float32),
    pltpu.VMEM((DEVICES, 2 * OWN, ROWS * PART), jnp.bfloat16),
]
SEMS = pltpu.SemaphoreType.DMA((STEPS,))


def inner_spectra(zh, own, coeffs, table):
    smem, vmem, hbm = (pl.BlockSpec(memory_space=m) for m in (pltpu.SMEM, pltpu.VMEM, pl.ANY))
    partial = (FRAME // 2 // LANES, 2, PART, ROWS, LANES)
    return pl.pallas_call(
        inner_kernel,
        in_specs=[smem, vmem, vmem, hbm],
        out_specs=[hbm, vmem, vmem],
        out_shape=[SPECTRA, pltpu.VMEM(table.shape, table.dtype), pltpu.VMEM(partial, jnp.float32)],
        scratch_shapes=SPECTRA_SCRATCH + [SEMS, SEMS],
        compiler_params=pltpu.CompilerParams(vmem_limit_bytes=20 << 20),
        cost_estimate=pl.CostEstimate(
            flops=2 * CHAN * FRAME * ROWS * PART, bytes_accessed=7 << 20, transcendentals=0
        ),
    )(zh, own, coeffs, pltpu.with_memory_space_constraint(table, pltpu.HBM))


def outer_spectra(zh, prev, following, coeffs, tables, partial, inner):
    smem, vmem, hbm = (pl.BlockSpec(memory_space=m) for m in (pltpu.SMEM, pltpu.VMEM, pl.ANY))
    return pl.pallas_call(
        outer_kernel,
        in_specs=[smem] + [vmem] * 5 + [hbm],
        out_specs=hbm,
        out_shape=SPECTRA,
        scratch_shapes=SPECTRA_SCRATCH + [SEMS],
        input_output_aliases={6: 0},
        compiler_params=pltpu.CompilerParams(vmem_limit_bytes=16 << 20),
        cost_estimate=pl.CostEstimate(
            flops=2 * CHAN * FRAME * ROWS * PART, bytes_accessed=7 << 20, transcendentals=0
        ),
    )(zh, following, prev, coeffs, resident(tables), resident(partial), inner)


def fit(values):
    nodes = (np.cos(np.pi * (np.arange(64) + 0.5) / 64) + 1.0) / 8.0
    return [float(v) for v in np.polynomial.Polynomial.fit(nodes, values(np.sqrt(nodes)), 5, domain=[0, 0.25], window=[0, 0.25]).coef]


COS = fit(lambda r: np.cos(2 * np.pi * r))
SIN = fit(lambda r: np.sin(2 * np.pi * r) / r)


def cos_sin(turns):
    rest = turns - jnp.round(turns)
    square = rest * rest
    cos, sin = COS[-1], SIN[-1]
    for a, b in zip(COS[-2::-1], SIN[-2::-1]):
        cos = cos * square + a
        sin = sin * square + b
    return cos, sin * rest


def input_order():
    order = np.arange(YX * ROWS).reshape(YX, ROWS).transpose(1, 0).reshape(-1)
    return (np.arange(YX * ROWS)[:, None] == order).astype(jnp.bfloat16)


def weights_kernel(first_ref, delays_hbm, order_hbm, out_ref, delays, delays_ref, order_ref, sems):
    copies = [
        pltpu.make_async_copy(delays_hbm, delays_ref, sems.at[0]),
        pltpu.make_async_copy(order_hbm, order_ref, sems.at[1]),
    ]
    for copy in copies:
        copy.start()
    for copy in copies:
        copy.wait()
    block = 128
    size = YX * ROWS

    def reorder(step, carry):
        at = pl.ds(pl.multiple_of(step * block, block), block)
        for group in range(INP):
            cut = slice(group * size, (group + 1) * size)
            rest = delays_ref[at, cut]
            total = jnp.zeros_like(rest)
            for _ in range(3):
                part = rest.astype(jnp.bfloat16)
                rest = rest - part.astype(jnp.float32)
                total = total + jnp.dot(part, order_ref[...], preferred_element_type=jnp.float32)
            delays[at, cut] = total * (1.0 / FRAME)
        return carry

    lax.fori_loop(0, BEAMS // block, reorder, 0)
    block = 16

    def rows(step, carry):
        at = pl.ds(pl.multiple_of(step * block, block), block)
        delay = delays[at]
        step_cos, step_sin = cos_sin(delay)
        cos, sin = cos_sin(delay * first_ref[0])
        for c in range(OWN):
            if c:
                cos, sin = cos * step_cos - sin * step_sin, sin * step_cos + cos * step_sin
            out_ref[c, 0, at] = cos.astype(jnp.bfloat16)
            out_ref[c, 1, at] = (-sin).astype(jnp.bfloat16)
        return carry

    lax.fori_loop(0, BEAMS // block, rows, 0)


def weights(first, delays):
    vmem = pl.BlockSpec(memory_space=pltpu.VMEM)
    return pl.pallas_call(
        weights_kernel,
        in_specs=[pl.BlockSpec(memory_space=m) for m in (pltpu.SMEM, pl.ANY, pl.ANY)],
        out_specs=vmem,
        out_shape=pltpu.VMEM((OWN, 2, BEAMS, INPUTS), jnp.bfloat16),
        scratch_shapes=[
            pltpu.VMEM((BEAMS, INPUTS), jnp.float32),
            pltpu.VMEM((BEAMS, INPUTS), jnp.float32),
            pltpu.VMEM((YX * ROWS, YX * ROWS), jnp.bfloat16),
            pltpu.SemaphoreType.DMA((2,)),
        ],
        compiler_params=pltpu.CompilerParams(vmem_limit_bytes=20 << 20),
        cost_estimate=pl.CostEstimate(
            flops=60 * BEAMS * INPUTS, bytes_accessed=12 << 20, transcendentals=0
        ),
    )(
        first,
        pltpu.with_memory_space_constraint(delays, pltpu.HBM),
        pltpu.with_memory_space_constraint(jnp.asarray(input_order()), pltpu.HBM),
    )


def arrange(wide, own, values):
    place = lax.broadcasted_iota(jnp.int32, (PLACES, LANES), 1) // PART
    rows = 2 * OWN
    halves = ROWS // GROUP
    for half in range(halves):
        for side in range(2):
            row = 4 * (own % 2) + 2 * (own // 2) + side
            a = [
                wide[half + (1 - inner) * halves, pl.ds(zh * PLACES * rows + row, PLACES, stride=rows), :].astype(
                    jnp.bfloat16
                )
                for zh in range(ZH)
                for inner in range(2)
            ]
            for bit in (1, 2, 4):
                moved = place & bit != 0
                a = [jnp.where(moved, a[(k + bit) % GROUP], a[k]) for k in range(GROUP)]
            for k in range(GROUP):
                value = a[-k % GROUP]
                value = pltpu.roll(value, LANES - k * PART, 1) if k else value
                for group in range(INP):
                    at = (group * ROWS + half * GROUP + k) * YX
                    cut = slice(side * LANES, (side + 1) * LANES)
                    values[at : at + YX, cut] = value[group * YX : (group + 1) * YX]


def beams_kernel(spectra_ref, weight, out_ref, wide, values, result, sems):
    for tile in range(ROWS * PLANE // LANES):
        part = spectra_ref[:, :, tile * LANES : (tile + 1) * LANES]
        wide[tile] = part.astype(jnp.float32).reshape(DEVICES * 2 * OWN, LANES)
    lane = lax.broadcasted_iota(jnp.int32, (BEAMS, LANES), 1)
    taken_over = lax.rem(lane, PLANE) < LATE
    copies = []
    for channel in range(OWN):
        arrange(wide, channel, values.at[channel])
        here = values[channel]
        by_re = jnp.dot(weight[channel, 0], here, preferred_element_type=jnp.float32)
        by_im = jnp.dot(weight[channel, 1], here, preferred_element_type=jnp.float32)
        parts = (by_re[:, :LANES] - by_im[:, LANES:], by_re[:, LANES:] + by_im[:, :LANES])
        for side, part in enumerate(parts):
            part = jnp.where(taken_over, pltpu.roll(part, PLANE, 1), part) * (1.0 / math.sqrt(INPUTS))
            result[side, channel] = part.astype(jnp.bfloat16)
        copies.append(pltpu.make_async_copy(result.at[:, channel], out_ref.at[:, channel], sems.at[channel]))
        copies[-1].start()
    for copy in copies:
        copy.wait()


def beams(received, weight):
    vmem = pl.BlockSpec(memory_space=pltpu.VMEM)
    shape = (2, OWN, BEAMS, FRAMES)
    return pl.pallas_call(
        beams_kernel,
        in_specs=[vmem, vmem],
        out_specs=pl.BlockSpec(memory_space=pl.ANY),
        out_shape=jax.ShapeDtypeStruct(shape, jnp.bfloat16),
        scratch_shapes=[
            pltpu.VMEM((ROWS * PLANE // LANES, DEVICES * 2 * OWN, LANES), jnp.float32),
            pltpu.VMEM((OWN, INPUTS, 2 * LANES), jnp.bfloat16),
            pltpu.VMEM(shape, jnp.bfloat16),
            pltpu.SemaphoreType.DMA((OWN,)),
        ],
        compiler_params=pltpu.CompilerParams(vmem_limit_bytes=20 << 20),
        cost_estimate=pl.CostEstimate(
            flops=8 * OWN * BEAMS * INPUTS * FRAMES, bytes_accessed=11 << 20, transcendentals=0
        ),
    )(received, resident(weight))


def body(samples, coeffs, delays):
    first = (lax.axis_index(ALL) * OWN).astype(jnp.float32).reshape(1)
    zh = lax.axis_index("zh").astype(jnp.int32).reshape(1)
    table = jnp.asarray(dft_tables())
    up = [(i, i + 1) for i in range(ZH - 1)]
    down = [(i, (i - 1) % ZH) for i in range(ZH)]

    own = lax.all_to_all(samples.reshape(YX, ROWS, 2 * FRAME), ("y", "x"), 0, 0, tiled=True)
    following = lax.ppermute(own[:HALO], "zh", down)
    last = own[YX - HALO :].reshape(HALO, ROWS, 2, FRAME)
    last = jnp.concatenate([last[:1, :, 1], last[1:].transpose(0, 2, 1, 3).reshape(LATE - 2, ROWS, FRAME)])
    prev = lax.ppermute(last, "zh", up)
    weight = weights(first, delays)
    inner, tables, partial = inner_spectra(zh, own, coeffs, table)
    following, weight = lax.optimization_barrier((following, weight))
    blocks = outer_spectra(zh, prev, following, coeffs, tables, partial, inner)
    received = lax.all_to_all(blocks, OWNERS, 0, 0, tiled=True)
    return beams(received, weight)


def solution(mesh):
    fine = Mesh(mesh.devices.reshape(4, 4, 4, 2, 2), ALL)
    in_specs = (P(("zl", "core"), ("zh", "y", "x")), P(), P())
    out_specs = P(None, ALL, None, None)
    return jax.shard_map(body, mesh=fine, in_specs=in_specs, out_specs=out_specs, check_vma=False)
```

```python
import math

import jax
import jax.numpy as jnp
import numpy as np
from jax import lax
from jax.experimental import pallas as pl
from jax.experimental.pallas import tpu as pltpu
from jax.sharding import Mesh
from jax.sharding import PartitionSpec as P

CHAN = 1024
FRAME = 2048
TAPS = 16
INPUTS = 1024
BEAMS = 512
FRAMES = 128

ZH, YX, INP, DEVICES = 4, 16, 4, 256
PLANE = FRAMES // ZH
LATE = 8
HALO = LATE // 2
PART = PLANE // 2
ROWS = INPUTS // INP // YX
OWN = CHAN // DEVICES
PLACES = YX * INP
LANES = 128
GROUP = LANES // PART
PITCH = PART + 8
ALL = ("zh", "y", "x", "zl", "core")
OWNERS = ("zh", "zl", "core", "y", "x")


def dft_tables():
    turn = np.arange(FRAME) * (2.0 * np.pi / FRAME)
    index = np.outer(np.arange(CHAN), np.arange(FRAME // 2)) % FRAME
    table = np.stack([np.cos(turn)[index], -np.sin(turn)[index]], axis=1)
    table = table.reshape(ZH, YX, INP, OWN // 2, 2, 2, FRAME // 2).transpose(4, 0, 2, 1, 3, 5, 6)
    return table.reshape(2, CHAN, FRAME // 2).astype(jnp.bfloat16)


def weighted(frame, taps, newest, delays):
    delays = list(delays)
    total = taps[delays[0]] * frame(newest - delays[0])
    for t in delays[1:]:
        total = total + taps[t] * frame(newest - t)
    return total


def resident(value):
    return pltpu.with_memory_space_constraint(value, pltpu.VMEM)


def transform(sums, tables, result, out_ref, lanes, out_sems, ready):
    steps = out_sems.shape[0]
    block = CHAN // steps
    upper = lax.broadcasted_iota(jnp.int32, (block // 8, 8, ROWS * PART), 1) < 4
    copies = []
    for step in range(steps):
        ready(step)
        cut = slice(step * block, (step + 1) * block)
        even, odd = (
            lax.dot_general(
                tables[k, cut], sums[k], (((1,), (1,)), ((), ())), preferred_element_type=jnp.float32
            ).reshape(block // 8, 8, ROWS * PART)
            * (1.0 / math.sqrt(FRAME))
            for k in range(2)
        )
        one = jnp.where(upper, even, pltpu.roll(odd, 4, 1)).astype(jnp.bfloat16)
        two = jnp.where(upper, pltpu.roll(even, 4, 1), odd).astype(jnp.bfloat16)
        for k in range(block // 8):
            result[step * block // 4 + 2 * k] = one[k]
            result[step * block // 4 + 2 * k + 1] = two[k]
        cut = pl.ds(step * block // 4, block // 4)
        copies.append(pltpu.make_async_copy(result.at[cut], out_ref.at[cut, :, lanes], out_sems.at[step]))
        copies[-1].start()
    for copy in copies:
        copy.wait()


def add_sums(sums, turned, step, shift):
    lanes = pl.ds(pl.multiple_of(step * LANES, LANES), LANES)
    for k in range(ROWS):
        first, second = (turned[side, k * PITCH : k * PITCH + PART] for side in range(2))
        to = k // GROUP * GROUP + lax.rem(k % GROUP + shift, GROUP)
        to = pl.ds(pl.multiple_of(to * PART, PART), PART)
        sums[0, to, lanes] = (first + second).astype(jnp.bfloat16)
        sums[1, to, lanes] = (first - second).astype(jnp.bfloat16)


def loader(ref, base):
    memo = {}

    def load(k):
        if k not in memo:
            memo[k] = ref[k // 2, :, pl.ds(base + (k % 2) * FRAME, LANES)].astype(jnp.float32)
        return memo[k]

    return load


def frame_loader(ref, base):
    memo = {}

    def load(k):
        if k not in memo:
            memo[k] = ref[k, :, pl.ds(base, LANES)].astype(jnp.float32)
        return memo[k]

    return load


def inner_kernel(zh_ref, own_ref, coeffs_ref, table_ref, out_ref, tables, partial_ref, *scratch):
    sums, turned, result, table_sems, out_sems = scratch
    steps = table_sems.shape[0]
    block = CHAN // steps
    keep = jnp.where(zh_ref[0] == ZH - 1, 0.0, 1.0)

    def table_copy(step):
        cut = pl.ds(step * block, block)
        return pltpu.make_async_copy(table_ref.at[:, cut], tables.at[:, cut], table_sems.at[step])

    for step in range(steps):
        table_copy(step).start()

    def tile(step, carry):
        for side in range(2):
            base = pl.multiple_of(step * LANES, LANES) + side * (FRAME // 2)
            own = loader(own_ref, base)
            taps = [coeffs_ref[t : t + 1, pl.ds(base, LANES)] for t in range(TAPS)]
            for j in range(LATE):
                partial_ref[step, side, LATE + j] = weighted(own, taps, LATE + j, range(LATE + j + 1))
            for j in range(PART):
                turned[side, pl.ds(j, ROWS, stride=PITCH), :] = weighted(own, taps, PART + j, range(TAPS))
            for j in range(LATE):
                part = weighted(own, taps, PLANE + j, range(j + 1, TAPS))
                partial_ref[step, side, j] = part * keep
        add_sums(sums, turned, step, 2 * zh_ref[0] + 1)
        return carry

    lax.fori_loop(0, FRAME // 2 // LANES, tile, 0)
    lanes = pl.ds(0, ROWS * PART)
    transform(sums, tables, result, out_ref, lanes, out_sems, lambda step: table_copy(step).wait())


def outer_kernel(zh_ref, next_ref, prev_ref, coeffs_ref, tables, partial_ref, _, out_ref, *scratch):
    sums, turned, result, out_sems = scratch

    def tile(step, carry):
        for side in range(2):
            base = pl.multiple_of(step * LANES, LANES) + side * (FRAME // 2)
            prev, following = frame_loader(prev_ref, base), loader(next_ref, base)
            taps = [coeffs_ref[t : t + 1, pl.ds(base, LANES)] for t in range(TAPS)]
            for j in range(LATE):
                total = partial_ref[step, side, j] + weighted(following, taps, j, range(j + 1))
                turned[side, pl.ds(j, ROWS, stride=PITCH), :] = total
                total = partial_ref[step, side, LATE + j]
                if LATE + j + 1 < TAPS:
                    total = total + weighted(prev, taps, 2 * LATE - 1 + j, range(LATE + j + 1, TAPS))
                turned[side, pl.ds(LATE + j, ROWS, stride=PITCH), :] = total
        add_sums(sums, turned, step, 2 * zh_ref[0])
        return carry

    lax.fori_loop(0, FRAME // 2 // LANES, tile, 0)
    lanes = pl.ds(ROWS * PART, ROWS * PART)
    transform(sums, tables, result, out_ref, lanes, out_sems, lambda step: None)


SPECTRA = jax.ShapeDtypeStruct((DEVICES, 2 * OWN, ROWS * PLANE), jnp.bfloat16)
STEPS = 4
SPECTRA_SCRATCH = [
    pltpu.VMEM((2, ROWS * PART, FRAME // 2), jnp.bfloat16),
    pltpu.VMEM((2, (ROWS + 1) * PITCH, LANES), jnp.float32),
    pltpu.VMEM((DEVICES, 2 * OWN, ROWS * PART), jnp.bfloat16),
]
SEMS = pltpu.SemaphoreType.DMA((STEPS,))


def inner_spectra(zh, own, coeffs, table):
    smem, vmem, hbm = (pl.BlockSpec(memory_space=m) for m in (pltpu.SMEM, pltpu.VMEM, pl.ANY))
    partial = (FRAME // 2 // LANES, 2, PART, ROWS, LANES)
    return pl.pallas_call(
        inner_kernel,
        in_specs=[smem, vmem, vmem, hbm],
        out_specs=[hbm, vmem, vmem],
        out_shape=[SPECTRA, pltpu.VMEM(table.shape, table.dtype), pltpu.VMEM(partial, jnp.float32)],
        scratch_shapes=SPECTRA_SCRATCH + [SEMS, SEMS],
        compiler_params=pltpu.CompilerParams(vmem_limit_bytes=20 << 20),
        cost_estimate=pl.CostEstimate(
            flops=2 * CHAN * FRAME * ROWS * PART, bytes_accessed=7 << 20, transcendentals=0
        ),
    )(zh, own, coeffs, pltpu.with_memory_space_constraint(table, pltpu.HBM))


def outer_spectra(zh, prev, following, coeffs, tables, partial, inner):
    smem, vmem, hbm = (pl.BlockSpec(memory_space=m) for m in (pltpu.SMEM, pltpu.VMEM, pl.ANY))
    return pl.pallas_call(
        outer_kernel,
        in_specs=[smem] + [vmem] * 5 + [hbm],
        out_specs=hbm,
        out_shape=SPECTRA,
        scratch_shapes=SPECTRA_SCRATCH + [SEMS],
        input_output_aliases={6: 0},
        compiler_params=pltpu.CompilerParams(vmem_limit_bytes=16 << 20),
        cost_estimate=pl.CostEstimate(
            flops=2 * CHAN * FRAME * ROWS * PART, bytes_accessed=7 << 20, transcendentals=0
        ),
    )(zh, following, prev, coeffs, resident(tables), resident(partial), inner)


def fit(values):
    nodes = (np.cos(np.pi * (np.arange(64) + 0.5) / 64) + 1.0) / 8.0
    return [float(v) for v in np.polynomial.Polynomial.fit(nodes, values(np.sqrt(nodes)), 5, domain=[0, 0.25], window=[0, 0.25]).coef]


COS = fit(lambda r: np.cos(2 * np.pi * r))
SIN = fit(lambda r: np.sin(2 * np.pi * r) / r)


def cos_sin(turns):
    rest = turns - jnp.round(turns)
    square = rest * rest
    cos, sin = COS[-1], SIN[-1]
    for a, b in zip(COS[-2::-1], SIN[-2::-1]):
        cos = cos * square + a
        sin = sin * square + b
    return cos, sin * rest


def input_order():
    order = np.arange(YX * ROWS).reshape(YX, ROWS).transpose(1, 0).reshape(-1)
    return (np.arange(YX * ROWS)[:, None] == order).astype(jnp.bfloat16)


def weights_kernel(first_ref, delays_hbm, order_hbm, out_ref, delays, delays_ref, order_ref, sems):
    copies = [
        pltpu.make_async_copy(delays_hbm, delays_ref, sems.at[0]),
        pltpu.make_async_copy(order_hbm, order_ref, sems.at[1]),
    ]
    for copy in copies:
        copy.start()
    for copy in copies:
        copy.wait()
    block = 128
    size = YX * ROWS

    def reorder(step, carry):
        at = pl.ds(pl.multiple_of(step * block, block), block)
        for group in range(INP):
            cut = slice(group * size, (group + 1) * size)
            rest = delays_ref[at, cut]
            total = jnp.zeros_like(rest)
            for _ in range(3):
                part = rest.astype(jnp.bfloat16)
                rest = rest - part.astype(jnp.float32)
                total = total + jnp.dot(part, order_ref[...], preferred_element_type=jnp.float32)
            delays[at, cut] = total * (1.0 / FRAME)
        return carry

    lax.fori_loop(0, BEAMS // block, reorder, 0)
    block = 16

    def rows(step, carry):
        at = pl.ds(pl.multiple_of(step * block, block), block)
        delay = delays[at]
        step_cos, step_sin = cos_sin(delay)
        cos, sin = cos_sin(delay * first_ref[0])
        for c in range(OWN):
            if c:
                cos, sin = cos * step_cos - sin * step_sin, sin * step_cos + cos * step_sin
            out_ref[c, 0, at] = cos.astype(jnp.bfloat16)
            out_ref[c, 1, at] = (-sin).astype(jnp.bfloat16)
        return carry

    lax.fori_loop(0, BEAMS // block, rows, 0)


def weights(first, delays):
    vmem = pl.BlockSpec(memory_space=pltpu.VMEM)
    return pl.pallas_call(
        weights_kernel,
        in_specs=[pl.BlockSpec(memory_space=m) for m in (pltpu.SMEM, pl.ANY, pl.ANY)],
        out_specs=vmem,
        out_shape=pltpu.VMEM((OWN, 2, BEAMS, INPUTS), jnp.bfloat16),
        scratch_shapes=[
            pltpu.VMEM((BEAMS, INPUTS), jnp.float32),
            pltpu.VMEM((BEAMS, INPUTS), jnp.float32),
            pltpu.VMEM((YX * ROWS, YX * ROWS), jnp.bfloat16),
            pltpu.SemaphoreType.DMA((2,)),
        ],
        compiler_params=pltpu.CompilerParams(vmem_limit_bytes=20 << 20),
        cost_estimate=pl.CostEstimate(
            flops=60 * BEAMS * INPUTS, bytes_accessed=12 << 20, transcendentals=0
        ),
    )(
        first,
        pltpu.with_memory_space_constraint(delays, pltpu.HBM),
        pltpu.with_memory_space_constraint(jnp.asarray(input_order()), pltpu.HBM),
    )


def arrange(wide, own, values):
    place = lax.broadcasted_iota(jnp.int32, (PLACES, LANES), 1) // PART
    rows = 2 * OWN
    halves = ROWS // GROUP
    for half in range(halves):
        for side in range(2):
            row = 4 * (own % 2) + 2 * (own // 2) + side
            a = [
                wide[half + (1 - inner) * halves, pl.ds(zh * PLACES * rows + row, PLACES, stride=rows), :].astype(
                    jnp.bfloat16
                )
                for zh in range(ZH)
                for inner in range(2)
            ]
            for bit in (1, 2, 4):
                moved = place & bit != 0
                a = [jnp.where(moved, a[(k + bit) % GROUP], a[k]) for k in range(GROUP)]
            for k in range(GROUP):
                value = a[-k % GROUP]
                value = pltpu.roll(value, LANES - k * PART, 1) if k else value
                for group in range(INP):
                    at = (group * ROWS + half * GROUP + k) * YX
                    cut = slice(side * LANES, (side + 1) * LANES)
                    values[at : at + YX, cut] = value[group * YX : (group + 1) * YX]


def beams_kernel(spectra_ref, weight, out_ref, wide, values, result, sems):
    for tile in range(ROWS * PLANE // LANES):
        part = spectra_ref[:, :, tile * LANES : (tile + 1) * LANES]
        wide[tile, : DEVICES * 2 * OWN] = part.astype(jnp.float32).reshape(DEVICES * 2 * OWN, LANES)
    lane = lax.broadcasted_iota(jnp.int32, (BEAMS, LANES), 1)
    taken_over = lax.rem(lane, PLANE) < LATE
    copies = []
    for channel in range(OWN):
        arrange(wide, channel, values.at[channel])
        here = values[channel]
        by_re = jnp.dot(weight[channel, 0], here, preferred_element_type=jnp.float32)
        by_im = jnp.dot(weight[channel, 1], here, preferred_element_type=jnp.float32)
        parts = (by_re[:, :LANES] - by_im[:, LANES:], by_re[:, LANES:] + by_im[:, :LANES])
        for side, part in enumerate(parts):
            part = jnp.where(taken_over, pltpu.roll(part, PLANE, 1), part) * (1.0 / math.sqrt(INPUTS))
            result[side, channel] = part.astype(jnp.bfloat16)
        copies.append(pltpu.make_async_copy(result.at[:, channel], out_ref.at[:, channel], sems.at[channel]))
        copies[-1].start()
    for copy in copies:
        copy.wait()


def beams(received, weight):
    vmem = pl.BlockSpec(memory_space=pltpu.VMEM)
    shape = (2, OWN, BEAMS, FRAMES)
    return pl.pallas_call(
        beams_kernel,
        in_specs=[vmem, vmem],
        out_specs=pl.BlockSpec(memory_space=pl.ANY),
        out_shape=jax.ShapeDtypeStruct(shape, jnp.bfloat16),
        scratch_shapes=[
            pltpu.VMEM((ROWS * PLANE // LANES, (DEVICES + 1) * 2 * OWN, LANES), jnp.float32),
            pltpu.VMEM((OWN, INPUTS, 2 * LANES), jnp.bfloat16),
            pltpu.VMEM(shape, jnp.bfloat16),
            pltpu.SemaphoreType.DMA((OWN,)),
        ],
        compiler_params=pltpu.CompilerParams(vmem_limit_bytes=20 << 20),
        cost_estimate=pl.CostEstimate(
            flops=8 * OWN * BEAMS * INPUTS * FRAMES, bytes_accessed=11 << 20, transcendentals=0
        ),
    )(received, resident(weight))


def body(samples, coeffs, delays):
    first = (lax.axis_index(ALL) * OWN).astype(jnp.float32).reshape(1)
    zh = lax.axis_index("zh").astype(jnp.int32).reshape(1)
    table = jnp.asarray(dft_tables())
    up = [(i, i + 1) for i in range(ZH - 1)]
    down = [(i, (i - 1) % ZH) for i in range(ZH)]

    own = lax.all_to_all(samples.reshape(YX, ROWS, 2 * FRAME), ("y", "x"), 0, 0, tiled=True)
    following = lax.ppermute(own[:HALO], "zh", down)
    last = own[YX - HALO :].reshape(HALO, ROWS, 2, FRAME)
    last = jnp.concatenate([last[:1, :, 1], last[1:].transpose(0, 2, 1, 3).reshape(LATE - 2, ROWS, FRAME)])
    prev = lax.ppermute(last, "zh", up)
    weight = weights(first, delays)
    inner, tables, partial = inner_spectra(zh, own, coeffs, table)
    following, weight = lax.optimization_barrier((following, weight))
    blocks = outer_spectra(zh, prev, following, coeffs, tables, partial, inner)
    received = lax.all_to_all(blocks, OWNERS, 0, 0, tiled=True)
    return beams(received, weight)


def solution(mesh):
    fine = Mesh(mesh.devices.reshape(4, 4, 4, 2, 2), ALL)
    in_specs = (P(("zl", "core"), ("zh", "y", "x")), P(), P())
    out_specs = P(None, ALL, None, None)
    return jax.shard_map(body, mesh=fine, in_specs=in_specs, out_specs=out_specs, check_vma=False)
```

```python
import math

import jax
import jax.numpy as jnp
import numpy as np
from jax import lax
from jax.experimental import pallas as pl
from jax.experimental.pallas import tpu as pltpu
from jax.sharding import Mesh
from jax.sharding import PartitionSpec as P

CHAN = 1024
FRAME = 2048
TAPS = 16
INPUTS = 1024
BEAMS = 512
FRAMES = 128

ZH, YX, INP, DEVICES = 4, 16, 4, 256
PLANE = FRAMES // ZH
LATE = 8
HALO = LATE // 2
PART = PLANE // 2
ROWS = INPUTS // INP // YX
OWN = CHAN // DEVICES
PLACES = YX * INP
LANES = 128
GROUP = LANES // PART
PITCH = PART + 8
ALL = ("zh", "y", "x", "zl", "core")
OWNERS = ("zh", "zl", "core", "y", "x")


def dft_tables():
    turn = np.arange(FRAME) * (2.0 * np.pi / FRAME)
    index = np.outer(np.arange(CHAN), np.arange(FRAME // 2)) % FRAME
    table = np.stack([np.cos(turn)[index], -np.sin(turn)[index]], axis=1)
    table = table.reshape(ZH, YX, INP, OWN // 2, 2, 2, FRAME // 2).transpose(4, 0, 2, 1, 3, 5, 6)
    return table.reshape(2, CHAN, FRAME // 2).astype(jnp.bfloat16)


def weighted(frame, taps, newest, delays):
    delays = list(delays)
    total = taps[delays[0]] * frame(newest - delays[0])
    for t in delays[1:]:
        total = total + taps[t] * frame(newest - t)
    return total


def resident(value):
    return pltpu.with_memory_space_constraint(value, pltpu.VMEM)


def transform(sums, tables, result, out_ref, lanes, out_sems, ready):
    steps = out_sems.shape[0]
    block = CHAN // steps
    upper = lax.broadcasted_iota(jnp.int32, (block // 8, 8, ROWS * PART), 1) < 4
    copies = []
    for step in range(steps):
        ready(step)
        cut = slice(step * block, (step + 1) * block)
        even, odd = (
            lax.dot_general(
                tables[k, cut], sums[k], (((1,), (1,)), ((), ())), preferred_element_type=jnp.float32
            ).reshape(block // 8, 8, ROWS * PART)
            * (1.0 / math.sqrt(FRAME))
            for k in range(2)
        )
        one = jnp.where(upper, even, pltpu.roll(odd, 4, 1)).astype(jnp.bfloat16)
        two = jnp.where(upper, pltpu.roll(even, 4, 1), odd).astype(jnp.bfloat16)
        for k in range(block // 8):
            result[step * block // 4 + 2 * k] = one[k]
            result[step * block // 4 + 2 * k + 1] = two[k]
        cut = pl.ds(step * block // 4, block // 4)
        copies.append(pltpu.make_async_copy(result.at[cut], out_ref.at[cut, :, lanes], out_sems.at[step]))
        copies[-1].start()
    for copy in copies:
        copy.wait()


def add_sums(sums, turned, step, shift):
    lanes = pl.ds(pl.multiple_of(step * LANES, LANES), LANES)
    for k in range(ROWS):
        first, second = (turned[side, k * PITCH : k * PITCH + PART] for side in range(2))
        to = k // GROUP * GROUP + lax.rem(k % GROUP + shift, GROUP)
        to = pl.ds(pl.multiple_of(to * PART, PART), PART)
        sums[0, to, lanes] = (first + second).astype(jnp.bfloat16)
        sums[1, to, lanes] = (first - second).astype(jnp.bfloat16)


def loader(ref, base):
    memo = {}

    def load(k):
        if k not in memo:
            memo[k] = ref[k // 2, :, pl.ds(base + (k % 2) * FRAME, LANES)].astype(jnp.float32)
        return memo[k]

    return load


def frame_loader(ref, base):
    memo = {}

    def load(k):
        if k not in memo:
            memo[k] = ref[k, :, pl.ds(base, LANES)].astype(jnp.float32)
        return memo[k]

    return load


def inner_kernel(zh_ref, own_ref, coeffs_ref, table_ref, out_ref, tables, partial_ref, *scratch):
    sums, turned, result, table_sems, out_sems = scratch
    steps = table_sems.shape[0]
    block = CHAN // steps
    keep = jnp.where(zh_ref[0] == ZH - 1, 0.0, 1.0)

    def table_copy(step):
        cut = pl.ds(step * block, block)
        return pltpu.make_async_copy(table_ref.at[:, cut], tables.at[:, cut], table_sems.at[step])

    for step in range(steps):
        table_copy(step).start()

    def tile(step, carry):
        for side in range(2):
            base = pl.multiple_of(step * LANES, LANES) + side * (FRAME // 2)
            own = loader(own_ref, base)
            taps = [coeffs_ref[t : t + 1, pl.ds(base, LANES)] for t in range(TAPS)]
            for j in range(LATE):
                partial_ref[step, side, LATE + j] = weighted(own, taps, LATE + j, range(LATE + j + 1))
            for j in range(PART):
                turned[side, pl.ds(j, ROWS, stride=PITCH), :] = weighted(own, taps, PART + j, range(TAPS))
            for j in range(LATE):
                part = weighted(own, taps, PLANE + j, range(j + 1, TAPS))
                partial_ref[step, side, j] = part * keep
        add_sums(sums, turned, step, 2 * zh_ref[0] + 1)
        return carry

    lax.fori_loop(0, FRAME // 2 // LANES, tile, 0)
    lanes = pl.ds(0, ROWS * PART)
    transform(sums, tables, result, out_ref, lanes, out_sems, lambda step: table_copy(step).wait())


def outer_kernel(zh_ref, next_ref, prev_ref, coeffs_ref, tables, partial_ref, _, out_ref, *scratch):
    sums, turned, result, out_sems = scratch

    def tile(step, carry):
        for side in range(2):
            base = pl.multiple_of(step * LANES, LANES) + side * (FRAME // 2)
            prev, following = frame_loader(prev_ref, base), loader(next_ref, base)
            taps = [coeffs_ref[t : t + 1, pl.ds(base, LANES)] for t in range(TAPS)]
            for j in range(LATE):
                total = partial_ref[step, side, j] + weighted(following, taps, j, range(j + 1))
                turned[side, pl.ds(j, ROWS, stride=PITCH), :] = total
                total = partial_ref[step, side, LATE + j]
                if LATE + j + 1 < TAPS:
                    total = total + weighted(prev, taps, 2 * LATE - 1 + j, range(LATE + j + 1, TAPS))
                turned[side, pl.ds(LATE + j, ROWS, stride=PITCH), :] = total
        add_sums(sums, turned, step, 2 * zh_ref[0])
        return carry

    lax.fori_loop(0, FRAME // 2 // LANES, tile, 0)
    lanes = pl.ds(ROWS * PART, ROWS * PART)
    transform(sums, tables, result, out_ref, lanes, out_sems, lambda step: None)


def ends_kernel(own_ref, first_ref, last_ref):
    first_ref[...] = own_ref[:HALO]
    for k in range(TAPS - 1 - LATE):
        f = PLANE - (TAPS - 1 - LATE) + k
        last_ref[k] = own_ref[f // 2, :, f % 2 * FRAME : (f % 2 + 1) * FRAME]


def ends(own):
    vmem = pl.BlockSpec(memory_space=pltpu.VMEM)
    shapes = (HALO, ROWS, 2 * FRAME), (TAPS - 1 - LATE, ROWS, FRAME)
    return pl.pallas_call(
        ends_kernel,
        in_specs=[vmem],
        out_specs=[vmem, vmem],
        out_shape=[jax.ShapeDtypeStruct(shape, own.dtype) for shape in shapes],
        compiler_params=pltpu.CompilerParams(vmem_limit_bytes=8 << 20),
        cost_estimate=pl.CostEstimate(flops=0, bytes_accessed=2 << 20, transcendentals=0),
    )(own)


SPECTRA = jax.ShapeDtypeStruct((DEVICES, 2 * OWN, ROWS * PLANE), jnp.bfloat16)
STEPS = 4
SPECTRA_SCRATCH = [
    pltpu.VMEM((2, ROWS * PART, FRAME // 2), jnp.bfloat16),
    pltpu.VMEM((2, (ROWS + 1) * PITCH, LANES), jnp.float32),
    pltpu.VMEM((DEVICES, 2 * OWN, ROWS * PART), jnp.bfloat16),
]
SEMS = pltpu.SemaphoreType.DMA((STEPS,))


def inner_spectra(zh, own, coeffs, table):
    smem, vmem, hbm = (pl.BlockSpec(memory_space=m) for m in (pltpu.SMEM, pltpu.VMEM, pl.ANY))
    partial = (FRAME // 2 // LANES, 2, PART, ROWS, LANES)
    return pl.pallas_call(
        inner_kernel,
        in_specs=[smem, vmem, vmem, hbm],
        out_specs=[hbm, vmem, vmem],
        out_shape=[SPECTRA, pltpu.VMEM(table.shape, table.dtype), pltpu.VMEM(partial, jnp.float32)],
        scratch_shapes=SPECTRA_SCRATCH + [SEMS, SEMS],
        compiler_params=pltpu.CompilerParams(vmem_limit_bytes=20 << 20),
        cost_estimate=pl.CostEstimate(
            flops=2 * CHAN * FRAME * ROWS * PART, bytes_accessed=7 << 20, transcendentals=0
        ),
    )(zh, own, coeffs, pltpu.with_memory_space_constraint(table, pltpu.HBM))


def outer_spectra(zh, prev, following, coeffs, tables, partial, inner):
    smem, vmem, hbm = (pl.BlockSpec(memory_space=m) for m in (pltpu.SMEM, pltpu.VMEM, pl.ANY))
    return pl.pallas_call(
        outer_kernel,
        in_specs=[smem] + [vmem] * 5 + [hbm],
        out_specs=hbm,
        out_shape=SPECTRA,
        scratch_shapes=SPECTRA_SCRATCH + [SEMS],
        input_output_aliases={6: 0},
        compiler_params=pltpu.CompilerParams(vmem_limit_bytes=16 << 20),
        cost_estimate=pl.CostEstimate(
            flops=2 * CHAN * FRAME * ROWS * PART, bytes_accessed=7 << 20, transcendentals=0
        ),
    )(zh, following, prev, coeffs, resident(tables), resident(partial), inner)


def fit(values):
    nodes = (np.cos(np.pi * (np.arange(64) + 0.5) / 64) + 1.0) / 8.0
    return [float(v) for v in np.polynomial.Polynomial.fit(nodes, values(np.sqrt(nodes)), 5, domain=[0, 0.25], window=[0, 0.25]).coef]


COS = fit(lambda r: np.cos(2 * np.pi * r))
SIN = fit(lambda r: np.sin(2 * np.pi * r) / r)


def cos_sin(turns):
    rest = turns - jnp.round(turns)
    square = rest * rest
    cos, sin = COS[-1], SIN[-1]
    for a, b in zip(COS[-2::-1], SIN[-2::-1]):
        cos = cos * square + a
        sin = sin * square + b
    return cos, sin * rest


def input_order():
    order = np.arange(YX * ROWS).reshape(YX, ROWS).transpose(1, 0).reshape(-1)
    return (np.arange(YX * ROWS)[:, None] == order).astype(jnp.bfloat16)


def weights_kernel(first_ref, delays_hbm, order_hbm, out_ref, delays, delays_ref, order_ref, sems):
    copies = [
        pltpu.make_async_copy(delays_hbm, delays_ref, sems.at[0]),
        pltpu.make_async_copy(order_hbm, order_ref, sems.at[1]),
    ]
    for copy in copies:
        copy.start()
    for copy in copies:
        copy.wait()
    block = 128
    size = YX * ROWS

    def reorder(step, carry):
        at = pl.ds(pl.multiple_of(step * block, block), block)
        for group in range(INP):
            cut = slice(group * size, (group + 1) * size)
            rest = delays_ref[at, cut]
            total = jnp.zeros_like(rest)
            for _ in range(3):
                part = rest.astype(jnp.bfloat16)
                rest = rest - part.astype(jnp.float32)
                total = total + jnp.dot(part, order_ref[...], preferred_element_type=jnp.float32)
            delays[at, cut] = total * (1.0 / FRAME)
        return carry

    lax.fori_loop(0, BEAMS // block, reorder, 0)
    block = 16

    def rows(step, carry):
        at = pl.ds(pl.multiple_of(step * block, block), block)
        delay = delays[at]
        step_cos, step_sin = cos_sin(delay)
        cos, sin = cos_sin(delay * first_ref[0])
        for c in range(OWN):
            if c:
                cos, sin = cos * step_cos - sin * step_sin, sin * step_cos + cos * step_sin
            out_ref[c, 0, at] = cos.astype(jnp.bfloat16)
            out_ref[c, 1, at] = (-sin).astype(jnp.bfloat16)
        return carry

    lax.fori_loop(0, BEAMS // block, rows, 0)


def weights(first, delays):
    vmem = pl.BlockSpec(memory_space=pltpu.VMEM)
    return pl.pallas_call(
        weights_kernel,
        in_specs=[pl.BlockSpec(memory_space=m) for m in (pltpu.SMEM, pl.ANY, pl.ANY)],
        out_specs=vmem,
        out_shape=pltpu.VMEM((OWN, 2, BEAMS, INPUTS), jnp.bfloat16),
        scratch_shapes=[
            pltpu.VMEM((BEAMS, INPUTS), jnp.float32),
            pltpu.VMEM((BEAMS, INPUTS), jnp.float32),
            pltpu.VMEM((YX * ROWS, YX * ROWS), jnp.bfloat16),
            pltpu.SemaphoreType.DMA((2,)),
        ],
        compiler_params=pltpu.CompilerParams(vmem_limit_bytes=20 << 20),
        cost_estimate=pl.CostEstimate(
            flops=60 * BEAMS * INPUTS, bytes_accessed=12 << 20, transcendentals=0
        ),
    )(
        first,
        pltpu.with_memory_space_constraint(delays, pltpu.HBM),
        pltpu.with_memory_space_constraint(jnp.asarray(input_order()), pltpu.HBM),
    )


def arrange(wide, own, values):
    place = lax.broadcasted_iota(jnp.int32, (PLACES, LANES), 1) // PART
    rows = 2 * OWN
    halves = ROWS // GROUP
    for half in range(halves):
        for side in range(2):
            row = 4 * (own % 2) + 2 * (own // 2) + side
            a = [
                wide[half + (1 - inner) * halves, pl.ds(zh * PLACES * rows + row, PLACES, stride=rows), :].astype(
                    jnp.bfloat16
                )
                for zh in range(ZH)
                for inner in range(2)
            ]
            for bit in (1, 2, 4):
                moved = place & bit != 0
                a = [jnp.where(moved, a[(k + bit) % GROUP], a[k]) for k in range(GROUP)]
            for k in range(GROUP):
                value = a[-k % GROUP]
                value = pltpu.roll(value, LANES - k * PART, 1) if k else value
                for group in range(INP):
                    at = (group * ROWS + half * GROUP + k) * YX
                    cut = slice(side * LANES, (side + 1) * LANES)
                    values[at : at + YX, cut] = value[group * YX : (group + 1) * YX]


def beams_kernel(spectra_ref, weight, out_ref, wide, values, result, sems):
    for tile in range(ROWS * PLANE // LANES):
        part = spectra_ref[:, :, tile * LANES : (tile + 1) * LANES]
        wide[tile, : DEVICES * 2 * OWN] = part.astype(jnp.float32).reshape(DEVICES * 2 * OWN, LANES)
    lane = lax.broadcasted_iota(jnp.int32, (BEAMS, LANES), 1)
    taken_over = lax.rem(lane, PLANE) < LATE
    copies = []
    for channel in range(OWN):
        arrange(wide, channel, values.at[channel])
        here = values[channel]
        by_re = jnp.dot(weight[channel, 0], here, preferred_element_type=jnp.float32)
        by_im = jnp.dot(weight[channel, 1], here, preferred_element_type=jnp.float32)
        parts = (by_re[:, :LANES] - by_im[:, LANES:], by_re[:, LANES:] + by_im[:, :LANES])
        for side, part in enumerate(parts):
            part = jnp.where(taken_over, pltpu.roll(part, PLANE, 1), part) * (1.0 / math.sqrt(INPUTS))
            result[side, channel] = part.astype(jnp.bfloat16)
        copies.append(pltpu.make_async_copy(result.at[:, channel], out_ref.at[:, channel], sems.at[channel]))
        copies[-1].start()
    for copy in copies:
        copy.wait()


def beams(received, weight):
    vmem = pl.BlockSpec(memory_space=pltpu.VMEM)
    shape = (2, OWN, BEAMS, FRAMES)
    return pl.pallas_call(
        beams_kernel,
        in_specs=[vmem, vmem],
        out_specs=pl.BlockSpec(memory_space=pl.ANY),
        out_shape=jax.ShapeDtypeStruct(shape, jnp.bfloat16),
        scratch_shapes=[
            pltpu.VMEM((ROWS * PLANE // LANES, (DEVICES + 1) * 2 * OWN, LANES), jnp.float32),
            pltpu.VMEM((OWN, INPUTS, 2 * LANES), jnp.bfloat16),
            pltpu.VMEM(shape, jnp.bfloat16),
            pltpu.SemaphoreType.DMA((OWN,)),
        ],
        compiler_params=pltpu.CompilerParams(vmem_limit_bytes=20 << 20),
        cost_estimate=pl.CostEstimate(
            flops=8 * OWN * BEAMS * INPUTS * FRAMES, bytes_accessed=11 << 20, transcendentals=0
        ),
    )(received, resident(weight))


def body(samples, coeffs, delays):
    first = (lax.axis_index(ALL) * OWN).astype(jnp.float32).reshape(1)
    zh = lax.axis_index("zh").astype(jnp.int32).reshape(1)
    table = jnp.asarray(dft_tables())
    up = [(i, i + 1) for i in range(ZH - 1)]
    down = [(i, (i - 1) % ZH) for i in range(ZH)]

    own = lax.all_to_all(samples.reshape(YX, ROWS, 2 * FRAME), ("y", "x"), 0, 0, tiled=True)
    down_frames, up_frames = ends(own)
    following = lax.ppermute(down_frames, "zh", down)
    prev = lax.ppermute(up_frames, "zh", up)
    weight = weights(first, delays)
    inner, tables, partial = inner_spectra(zh, own, coeffs, table)
    following, weight = lax.optimization_barrier((following, weight))
    blocks = outer_spectra(zh, prev, following, coeffs, tables, partial, inner)
    received = lax.all_to_all(blocks, OWNERS, 0, 0, tiled=True)
    return beams(received, weight)


def solution(mesh):
    fine = Mesh(mesh.devices.reshape(4, 4, 4, 2, 2), ALL)
    in_specs = (P(("zl", "core"), ("zh", "y", "x")), P(), P())
    out_specs = P(None, ALL, None, None)
    return jax.shard_map(body, mesh=fine, in_specs=in_specs, out_specs=out_specs, check_vma=False)
```

```python
import math

import jax
import jax.numpy as jnp
import numpy as np
from jax import lax
from jax.experimental import pallas as pl
from jax.experimental.pallas import tpu as pltpu
from jax.sharding import Mesh
from jax.sharding import PartitionSpec as P

CHAN = 1024
FRAME = 2048
TAPS = 16
INPUTS = 1024
BEAMS = 512
FRAMES = 128

ZH, YX, INP, DEVICES = 4, 16, 4, 256
PLANE = FRAMES // ZH
LATE = 8
HALO = LATE // 2
PART = PLANE // 2
ROWS = INPUTS // INP // YX
OWN = CHAN // DEVICES
PLACES = YX * INP
LANES = 128
GROUP = LANES // PART
PITCH = PART + 8
ALL = ("zh", "y", "x", "zl", "core")
OWNERS = ("zh", "zl", "core", "y", "x")


def dft_tables():
    turn = np.arange(FRAME) * (2.0 * np.pi / FRAME)
    index = np.outer(np.arange(CHAN), np.arange(FRAME // 2)) % FRAME
    table = np.stack([np.cos(turn)[index], -np.sin(turn)[index]], axis=1)
    table = table.reshape(ZH, YX, INP, OWN // 2, 2, 2, FRAME // 2).transpose(4, 0, 2, 1, 3, 5, 6)
    return table.reshape(2, CHAN, FRAME // 2).astype(jnp.bfloat16)


def weighted(frame, taps, newest, delays):
    delays = list(delays)
    total = taps[delays[0]] * frame(newest - delays[0])
    for t in delays[1:]:
        total = total + taps[t] * frame(newest - t)
    return total


def resident(value):
    return pltpu.with_memory_space_constraint(value, pltpu.VMEM)


def transform(sums, tables, result, out_ref, lanes, out_sems, ready):
    steps = out_sems.shape[0]
    block = CHAN // steps
    upper = lax.broadcasted_iota(jnp.int32, (block // 8, 8, ROWS * PART), 1) < 4
    copies = []
    for step in range(steps):
        ready(step)
        cut = slice(step * block, (step + 1) * block)
        even, odd = (
            lax.dot_general(
                tables[k, cut], sums[k], (((1,), (1,)), ((), ())), preferred_element_type=jnp.float32
            ).reshape(block // 8, 8, ROWS * PART)
            * (1.0 / math.sqrt(FRAME))
            for k in range(2)
        )
        one = jnp.where(upper, even, pltpu.roll(odd, 4, 1)).astype(jnp.bfloat16)
        two = jnp.where(upper, pltpu.roll(even, 4, 1), odd).astype(jnp.bfloat16)
        for k in range(block // 8):
            result[step * block // 4 + 2 * k] = one[k]
            result[step * block // 4 + 2 * k + 1] = two[k]
        cut = pl.ds(step * block // 4, block // 4)
        copies.append(pltpu.make_async_copy(result.at[cut], out_ref.at[cut, :, lanes], out_sems.at[step]))
        copies[-1].start()
    for copy in copies:
        copy.wait()


def add_sums(sums, turned, step, shift):
    lanes = pl.ds(pl.multiple_of(step * LANES, LANES), LANES)
    for k in range(ROWS):
        first, second = (turned[side, k * PITCH : k * PITCH + PART] for side in range(2))
        to = k // GROUP * GROUP + lax.rem(k % GROUP + shift, GROUP)
        to = pl.ds(pl.multiple_of(to * PART, PART), PART)
        sums[0, to, lanes] = (first + second).astype(jnp.bfloat16)
        sums[1, to, lanes] = (first - second).astype(jnp.bfloat16)


def loader(ref, base):
    memo = {}

    def load(k):
        if k not in memo:
            memo[k] = ref[k // 2, :, pl.ds(base + (k % 2) * FRAME, LANES)].astype(jnp.float32)
        return memo[k]

    return load


def frame_loader(ref, base):
    memo = {}

    def load(k):
        if k not in memo:
            memo[k] = ref[k, :, pl.ds(base, LANES)].astype(jnp.float32)
        return memo[k]

    return load


def inner_kernel(zh_ref, own_ref, coeffs_ref, table_ref, out_ref, tables, partial_ref, *scratch):
    sums, turned, result, table_sems, out_sems = scratch
    steps = table_sems.shape[0]
    block = CHAN // steps
    keep = jnp.where(zh_ref[0] == ZH - 1, 0.0, 1.0)

    def table_copy(step):
        cut = pl.ds(step * block, block)
        return pltpu.make_async_copy(table_ref.at[:, cut], tables.at[:, cut], table_sems.at[step])

    for step in range(steps):
        table_copy(step).start()

    def tile(step, carry):
        for side in range(2):
            base = pl.multiple_of(step * LANES, LANES) + side * (FRAME // 2)
            own = loader(own_ref, base)
            taps = [coeffs_ref[t : t + 1, pl.ds(base, LANES)] for t in range(TAPS)]
            for j in range(LATE):
                partial_ref[step, side, LATE + j] = weighted(own, taps, LATE + j, range(LATE + j + 1))
            for j in range(PART):
                turned[side, pl.ds(j, ROWS, stride=PITCH), :] = weighted(own, taps, PART + j, range(TAPS))
            for j in range(LATE):
                part = weighted(own, taps, PLANE + j, range(j + 1, TAPS))
                partial_ref[step, side, j] = part * keep
        add_sums(sums, turned, step, 2 * zh_ref[0] + 1)
        return carry

    lax.fori_loop(0, FRAME // 2 // LANES, tile, 0)
    lanes = pl.ds(0, ROWS * PART)
    transform(sums, tables, result, out_ref, lanes, out_sems, lambda step: table_copy(step).wait())


def outer_kernel(zh_ref, next_ref, prev_ref, coeffs_ref, tables, partial_ref, _, out_ref, *scratch):
    sums, turned, result, out_sems = scratch

    def tile(step, carry):
        for side in range(2):
            base = pl.multiple_of(step * LANES, LANES) + side * (FRAME // 2)
            prev, following = frame_loader(prev_ref, base), loader(next_ref, base)
            taps = [coeffs_ref[t : t + 1, pl.ds(base, LANES)] for t in range(TAPS)]
            for j in range(LATE):
                total = partial_ref[step, side, j] + weighted(following, taps, j, range(j + 1))
                turned[side, pl.ds(j, ROWS, stride=PITCH), :] = total
                total = partial_ref[step, side, LATE + j]
                if LATE + j + 1 < TAPS:
                    total = total + weighted(prev, taps, 2 * LATE - 1 + j, range(LATE + j + 1, TAPS))
                turned[side, pl.ds(LATE + j, ROWS, stride=PITCH), :] = total
        add_sums(sums, turned, step, 2 * zh_ref[0])
        return carry

    lax.fori_loop(0, FRAME // 2 // LANES, tile, 0)
    lanes = pl.ds(ROWS * PART, ROWS * PART)
    transform(sums, tables, result, out_ref, lanes, out_sems, lambda step: None)


def ends_kernel(own_ref, first_ref, last_ref):
    first_ref[...] = own_ref[:HALO]
    for k in range(TAPS - 1 - LATE):
        f = PLANE - (TAPS - 1 - LATE) + k
        last_ref[k] = own_ref[f // 2, :, f % 2 * FRAME : (f % 2 + 1) * FRAME]


def ends(own):
    vmem = pl.BlockSpec(memory_space=pltpu.VMEM)
    shapes = (HALO, ROWS, 2 * FRAME), (TAPS - 1 - LATE, ROWS, FRAME)
    return pl.pallas_call(
        ends_kernel,
        in_specs=[vmem],
        out_specs=[vmem, vmem],
        out_shape=[jax.ShapeDtypeStruct(shape, own.dtype) for shape in shapes],
        compiler_params=pltpu.CompilerParams(vmem_limit_bytes=8 << 20),
        cost_estimate=pl.CostEstimate(flops=0, bytes_accessed=2 << 20, transcendentals=0),
    )(own)


SPECTRA = jax.ShapeDtypeStruct((DEVICES, 2 * OWN, ROWS * PLANE), jnp.bfloat16)
STEPS = 2
SPECTRA_SCRATCH = [
    pltpu.VMEM((2, ROWS * PART, FRAME // 2), jnp.bfloat16),
    pltpu.VMEM((2, (ROWS + 1) * PITCH, LANES), jnp.float32),
    pltpu.VMEM((DEVICES, 2 * OWN, ROWS * PART), jnp.bfloat16),
]
SEMS = pltpu.SemaphoreType.DMA((STEPS,))


def inner_spectra(zh, own, coeffs, table):
    smem, vmem, hbm = (pl.BlockSpec(memory_space=m) for m in (pltpu.SMEM, pltpu.VMEM, pl.ANY))
    partial = (FRAME // 2 // LANES, 2, PART, ROWS, LANES)
    return pl.pallas_call(
        inner_kernel,
        in_specs=[smem, vmem, vmem, hbm],
        out_specs=[hbm, vmem, vmem],
        out_shape=[SPECTRA, pltpu.VMEM(table.shape, table.dtype), pltpu.VMEM(partial, jnp.float32)],
        scratch_shapes=SPECTRA_SCRATCH + [SEMS, SEMS],
        compiler_params=pltpu.CompilerParams(vmem_limit_bytes=20 << 20),
        cost_estimate=pl.CostEstimate(
            flops=2 * CHAN * FRAME * ROWS * PART, bytes_accessed=7 << 20, transcendentals=0
        ),
    )(zh, own, coeffs, pltpu.with_memory_space_constraint(table, pltpu.HBM))


def outer_spectra(zh, prev, following, coeffs, tables, partial, inner):
    smem, vmem, hbm = (pl.BlockSpec(memory_space=m) for m in (pltpu.SMEM, pltpu.VMEM, pl.ANY))
    return pl.pallas_call(
        outer_kernel,
        in_specs=[smem] + [vmem] * 5 + [hbm],
        out_specs=hbm,
        out_shape=SPECTRA,
        scratch_shapes=SPECTRA_SCRATCH + [SEMS],
        input_output_aliases={6: 0},
        compiler_params=pltpu.CompilerParams(vmem_limit_bytes=16 << 20),
        cost_estimate=pl.CostEstimate(
            flops=2 * CHAN * FRAME * ROWS * PART, bytes_accessed=7 << 20, transcendentals=0
        ),
    )(zh, following, prev, coeffs, resident(tables), resident(partial), inner)


def fit(values):
    nodes = (np.cos(np.pi * (np.arange(64) + 0.5) / 64) + 1.0) / 8.0
    return [float(v) for v in np.polynomial.Polynomial.fit(nodes, values(np.sqrt(nodes)), 5, domain=[0, 0.25], window=[0, 0.25]).coef]


COS = fit(lambda r: np.cos(2 * np.pi * r))
SIN = fit(lambda r: np.sin(2 * np.pi * r) / r)


def cos_sin(turns):
    rest = turns - jnp.round(turns)
    square = rest * rest
    cos, sin = COS[-1], SIN[-1]
    for a, b in zip(COS[-2::-1], SIN[-2::-1]):
        cos = cos * square + a
        sin = sin * square + b
    return cos, sin * rest


def input_order():
    order = np.arange(YX * ROWS).reshape(YX, ROWS).transpose(1, 0).reshape(-1)
    return (np.arange(YX * ROWS)[:, None] == order).astype(jnp.bfloat16)


def weights_kernel(first_ref, delays_hbm, order_hbm, out_ref, delays, delays_ref, order_ref, sems):
    copies = [
        pltpu.make_async_copy(delays_hbm, delays_ref, sems.at[0]),
        pltpu.make_async_copy(order_hbm, order_ref, sems.at[1]),
    ]
    for copy in copies:
        copy.start()
    for copy in copies:
        copy.wait()
    block = 128
    size = YX * ROWS

    def reorder(step, carry):
        at = pl.ds(pl.multiple_of(step * block, block), block)
        for group in range(INP):
            cut = slice(group * size, (group + 1) * size)
            rest = delays_ref[at, cut]
            total = jnp.zeros_like(rest)
            for _ in range(3):
                part = rest.astype(jnp.bfloat16)
                rest = rest - part.astype(jnp.float32)
                total = total + jnp.dot(part, order_ref[...], preferred_element_type=jnp.float32)
            delays[at, cut] = total * (1.0 / FRAME)
        return carry

    lax.fori_loop(0, BEAMS // block, reorder, 0)
    block = 16

    def rows(step, carry):
        at = pl.ds(pl.multiple_of(step * block, block), block)
        delay = delays[at]
        step_cos, step_sin = cos_sin(delay)
        cos, sin = cos_sin(delay * first_ref[0])
        for c in range(OWN):
            if c:
                cos, sin = cos * step_cos - sin * step_sin, sin * step_cos + cos * step_sin
            out_ref[c, 0, at] = cos.astype(jnp.bfloat16)
            out_ref[c, 1, at] = (-sin).astype(jnp.bfloat16)
        return carry

    lax.fori_loop(0, BEAMS // block, rows, 0)


def weights(first, delays):
    vmem = pl.BlockSpec(memory_space=pltpu.VMEM)
    return pl.pallas_call(
        weights_kernel,
        in_specs=[pl.BlockSpec(memory_space=m) for m in (pltpu.SMEM, pl.ANY, pl.ANY)],
        out_specs=vmem,
        out_shape=pltpu.VMEM((OWN, 2, BEAMS, INPUTS), jnp.bfloat16),
        scratch_shapes=[
            pltpu.VMEM((BEAMS, INPUTS), jnp.float32),
            pltpu.VMEM((BEAMS, INPUTS), jnp.float32),
            pltpu.VMEM((YX * ROWS, YX * ROWS), jnp.bfloat16),
            pltpu.SemaphoreType.DMA((2,)),
        ],
        compiler_params=pltpu.CompilerParams(vmem_limit_bytes=20 << 20),
        cost_estimate=pl.CostEstimate(
            flops=60 * BEAMS * INPUTS, bytes_accessed=12 << 20, transcendentals=0
        ),
    )(
        first,
        pltpu.with_memory_space_constraint(delays, pltpu.HBM),
        pltpu.with_memory_space_constraint(jnp.asarray(input_order()), pltpu.HBM),
    )


def arrange(wide, own, values):
    place = lax.broadcasted_iota(jnp.int32, (PLACES, LANES), 1) // PART
    rows = 2 * OWN
    halves = ROWS // GROUP
    for half in range(halves):
        for side in range(2):
            row = 4 * (own % 2) + 2 * (own // 2) + side
            a = [
                wide[half + (1 - inner) * halves, pl.ds(zh * PLACES * rows + row, PLACES, stride=rows), :].astype(
                    jnp.bfloat16
                )
                for zh in range(ZH)
                for inner in range(2)
            ]
            for bit in (1, 2, 4):
                moved = place & bit != 0
                a = [jnp.where(moved, a[(k + bit) % GROUP], a[k]) for k in range(GROUP)]
            for k in range(GROUP):
                value = a[-k % GROUP]
                value = pltpu.roll(value, LANES - k * PART, 1) if k else value
                for group in range(INP):
                    at = (group * ROWS + half * GROUP + k) * YX
                    cut = slice(side * LANES, (side + 1) * LANES)
                    values[at : at + YX, cut] = value[group * YX : (group + 1) * YX]


def beams_kernel(spectra_ref, weight, out_ref, wide, values, result, sems):
    for tile in range(ROWS * PLANE // LANES):
        part = spectra_ref[:, :, tile * LANES : (tile + 1) * LANES]
        wide[tile, : DEVICES * 2 * OWN] = part.astype(jnp.float32).reshape(DEVICES * 2 * OWN, LANES)
    lane = lax.broadcasted_iota(jnp.int32, (BEAMS, LANES), 1)
    taken_over = lax.rem(lane, PLANE) < LATE
    copies = []
    for channel in range(OWN):
        arrange(wide, channel, values.at[channel])
        here = values[channel]
        by_re = jnp.dot(weight[channel, 0], here, preferred_element_type=jnp.float32)
        by_im = jnp.dot(weight[channel, 1], here, preferred_element_type=jnp.float32)
        parts = (by_re[:, :LANES] - by_im[:, LANES:], by_re[:, LANES:] + by_im[:, :LANES])
        for side, part in enumerate(parts):
            part = jnp.where(taken_over, pltpu.roll(part, PLANE, 1), part) * (1.0 / math.sqrt(INPUTS))
            result[side, channel] = part.astype(jnp.bfloat16)
        copies.append(pltpu.make_async_copy(result.at[:, channel], out_ref.at[:, channel], sems.at[channel]))
        copies[-1].start()
    for copy in copies:
        copy.wait()


def beams(received, weight):
    vmem = pl.BlockSpec(memory_space=pltpu.VMEM)
    shape = (2, OWN, BEAMS, FRAMES)
    return pl.pallas_call(
        beams_kernel,
        in_specs=[vmem, vmem],
        out_specs=pl.BlockSpec(memory_space=pl.ANY),
        out_shape=jax.ShapeDtypeStruct(shape, jnp.bfloat16),
        scratch_shapes=[
            pltpu.VMEM((ROWS * PLANE // LANES, (DEVICES + 1) * 2 * OWN, LANES), jnp.float32),
            pltpu.VMEM((OWN, INPUTS, 2 * LANES), jnp.bfloat16),
            pltpu.VMEM(shape, jnp.bfloat16),
            pltpu.SemaphoreType.DMA((OWN,)),
        ],
        compiler_params=pltpu.CompilerParams(vmem_limit_bytes=20 << 20),
        cost_estimate=pl.CostEstimate(
            flops=8 * OWN * BEAMS * INPUTS * FRAMES, bytes_accessed=11 << 20, transcendentals=0
        ),
    )(received, resident(weight))


def body(samples, coeffs, delays):
    first = (lax.axis_index(ALL) * OWN).astype(jnp.float32).reshape(1)
    zh = lax.axis_index("zh").astype(jnp.int32).reshape(1)
    table = jnp.asarray(dft_tables())
    up = [(i, i + 1) for i in range(ZH - 1)]
    down = [(i, (i - 1) % ZH) for i in range(ZH)]

    own = lax.all_to_all(samples.reshape(YX, ROWS, 2 * FRAME), ("y", "x"), 0, 0, tiled=True)
    down_frames, up_frames = ends(own)
    following = lax.ppermute(down_frames, "zh", down)
    prev = lax.ppermute(up_frames, "zh", up)
    weight = weights(first, delays)
    inner, tables, partial = inner_spectra(zh, own, coeffs, table)
    following, weight = lax.optimization_barrier((following, weight))
    blocks = outer_spectra(zh, prev, following, coeffs, tables, partial, inner)
    received = lax.all_to_all(blocks, OWNERS, 0, 0, tiled=True)
    return beams(received, weight)


def solution(mesh):
    fine = Mesh(mesh.devices.reshape(4, 4, 4, 2, 2), ALL)
    in_specs = (P(("zl", "core"), ("zh", "y", "x")), P(), P())
    out_specs = P(None, ALL, None, None)
    return jax.shard_map(body, mesh=fine, in_specs=in_specs, out_specs=out_specs, check_vma=False)
```

```python
import math

import jax
import jax.numpy as jnp
import numpy as np
from jax import lax
from jax.experimental import pallas as pl
from jax.experimental.pallas import tpu as pltpu
from jax.sharding import Mesh
from jax.sharding import PartitionSpec as P

CHAN = 1024
FRAME = 2048
TAPS = 16
INPUTS = 1024
BEAMS = 512
FRAMES = 128

ZH, YX, INP, DEVICES = 4, 16, 4, 256
PLANE = FRAMES // ZH
LATE = 8
HALO = LATE // 2
PART = PLANE // 2
ROWS = INPUTS // INP // YX
OWN = CHAN // DEVICES
PLACES = YX * INP
LANES = 128
GROUP = LANES // PART
PITCH = PART + 8
ALL = ("zh", "y", "x", "zl", "core")
OWNERS = ("zh", "zl", "core", "y", "x")


def dft_tables():
    turn = np.arange(FRAME) * (2.0 * np.pi / FRAME)
    index = np.outer(np.arange(CHAN), np.arange(FRAME // 2)) % FRAME
    table = np.stack([np.cos(turn)[index], -np.sin(turn)[index]], axis=1)
    table = table.reshape(ZH, YX, INP, OWN // 2, 2, 2, FRAME // 2).transpose(4, 0, 2, 1, 3, 5, 6)
    return table.reshape(2, CHAN, FRAME // 2).astype(jnp.bfloat16)


def weighted(frame, taps, newest, delays):
    delays = list(delays)
    total = taps[delays[0]] * frame(newest - delays[0])
    for t in delays[1:]:
        total = total + taps[t] * frame(newest - t)
    return total


def resident(value):
    return pltpu.with_memory_space_constraint(value, pltpu.VMEM)


def transform(sums, tables, result, out_ref, lanes, out_sems, ready):
    steps = out_sems.shape[0]
    block = CHAN // steps
    upper = lax.broadcasted_iota(jnp.int32, (block // 8, 8, ROWS * PART), 1) < 4
    copies = []
    for step in range(steps):
        ready(step)
        cut = slice(step * block, (step + 1) * block)
        even, odd = (
            lax.dot_general(
                tables[k, cut], sums[k], (((1,), (1,)), ((), ())), preferred_element_type=jnp.float32
            ).reshape(block // 8, 8, ROWS * PART)
            * (1.0 / math.sqrt(FRAME))
            for k in range(2)
        )
        one = jnp.where(upper, even, pltpu.roll(odd, 4, 1)).astype(jnp.bfloat16)
        two = jnp.where(upper, pltpu.roll(even, 4, 1), odd).astype(jnp.bfloat16)
        for k in range(block // 8):
            result[step * block // 4 + 2 * k] = one[k]
            result[step * block // 4 + 2 * k + 1] = two[k]
        cut = pl.ds(step * block // 4, block // 4)
        copies.append(pltpu.make_async_copy(result.at[cut], out_ref.at[cut, :, lanes], out_sems.at[step]))
        copies[-1].start()
    for copy in copies:
        copy.wait()


def add_sums(sums, turned, step, shift):
    lanes = pl.ds(pl.multiple_of(step * LANES, LANES), LANES)
    for k in range(ROWS):
        first, second = (turned[side, k * PITCH : k * PITCH + PART] for side in range(2))
        to = k // GROUP * GROUP + lax.rem(k % GROUP + shift, GROUP)
        to = pl.ds(pl.multiple_of(to * PART, PART), PART)
        sums[0, to, lanes] = (first + second).astype(jnp.bfloat16)
        sums[1, to, lanes] = (first - second).astype(jnp.bfloat16)


def loader(ref, base):
    memo = {}

    def load(k):
        if k not in memo:
            memo[k] = ref[k // 2, :, pl.ds(base + (k % 2) * FRAME, LANES)].astype(jnp.float32)
        return memo[k]

    return load


def frame_loader(ref, base):
    memo = {}

    def load(k):
        if k not in memo:
            memo[k] = ref[k, :, pl.ds(base, LANES)].astype(jnp.float32)
        return memo[k]

    return load


def inner_kernel(zh_ref, own_ref, coeffs_ref, table_ref, out_ref, tables, partial_ref, *scratch):
    sums, turned, result, table_sems, out_sems = scratch
    steps = table_sems.shape[0]
    block = CHAN // steps
    keep = jnp.where(zh_ref[0] == ZH - 1, 0.0, 1.0)

    def table_copy(step):
        cut = pl.ds(step * block, block)
        return pltpu.make_async_copy(table_ref.at[:, cut], tables.at[:, cut], table_sems.at[step])

    for step in range(steps):
        table_copy(step).start()

    def tile(step, carry):
        for side in range(2):
            base = pl.multiple_of(step * LANES, LANES) + side * (FRAME // 2)
            own = loader(own_ref, base)
            taps = [coeffs_ref[t : t + 1, pl.ds(base, LANES)] for t in range(TAPS)]
            for j in range(LATE):
                partial_ref[step, side, LATE + j] = weighted(own, taps, LATE + j, range(LATE + j + 1))
            for j in range(PART):
                turned[side, pl.ds(j, ROWS, stride=PITCH), :] = weighted(own, taps, PART + j, range(TAPS))
            for j in range(LATE):
                part = weighted(own, taps, PLANE + j, range(j + 1, TAPS))
                partial_ref[step, side, j] = part * keep
        add_sums(sums, turned, step, 2 * zh_ref[0] + 1)
        return carry

    lax.fori_loop(0, FRAME // 2 // LANES, tile, 0)
    lanes = pl.ds(0, ROWS * PART)
    transform(sums, tables, result, out_ref, lanes, out_sems, lambda step: table_copy(step).wait())


def outer_kernel(zh_ref, next_ref, prev_ref, coeffs_ref, tables, partial_ref, _, out_ref, *scratch):
    sums, turned, result, out_sems = scratch

    def tile(step, carry):
        for side in range(2):
            base = pl.multiple_of(step * LANES, LANES) + side * (FRAME // 2)
            prev, following = frame_loader(prev_ref, base), loader(next_ref, base)
            taps = [coeffs_ref[t : t + 1, pl.ds(base, LANES)] for t in range(TAPS)]
            for j in range(LATE):
                total = partial_ref[step, side, j] + weighted(following, taps, j, range(j + 1))
                turned[side, pl.ds(j, ROWS, stride=PITCH), :] = total
                total = partial_ref[step, side, LATE + j]
                if LATE + j + 1 < TAPS:
                    total = total + weighted(prev, taps, 2 * LATE - 1 + j, range(LATE + j + 1, TAPS))
                turned[side, pl.ds(LATE + j, ROWS, stride=PITCH), :] = total
        add_sums(sums, turned, step, 2 * zh_ref[0])
        return carry

    lax.fori_loop(0, FRAME // 2 // LANES, tile, 0, unroll=2)
    lanes = pl.ds(ROWS * PART, ROWS * PART)
    transform(sums, tables, result, out_ref, lanes, out_sems, lambda step: None)


def ends_kernel(own_ref, first_ref, last_ref):
    first_ref[...] = own_ref[:HALO]
    for k in range(TAPS - 1 - LATE):
        f = PLANE - (TAPS - 1 - LATE) + k
        last_ref[k] = own_ref[f // 2, :, f % 2 * FRAME : (f % 2 + 1) * FRAME]


def ends(own):
    vmem = pl.BlockSpec(memory_space=pltpu.VMEM)
    shapes = (HALO, ROWS, 2 * FRAME), (TAPS - 1 - LATE, ROWS, FRAME)
    return pl.pallas_call(
        ends_kernel,
        in_specs=[vmem],
        out_specs=[vmem, vmem],
        out_shape=[jax.ShapeDtypeStruct(shape, own.dtype) for shape in shapes],
        compiler_params=pltpu.CompilerParams(vmem_limit_bytes=8 << 20),
        cost_estimate=pl.CostEstimate(flops=0, bytes_accessed=2 << 20, transcendentals=0),
    )(own)


SPECTRA = jax.ShapeDtypeStruct((DEVICES, 2 * OWN, ROWS * PLANE), jnp.bfloat16)
STEPS = 2
SPECTRA_SCRATCH = [
    pltpu.VMEM((2, ROWS * PART, FRAME // 2), jnp.bfloat16),
    pltpu.VMEM((2, (ROWS + 1) * PITCH, LANES), jnp.float32),
    pltpu.VMEM((DEVICES, 2 * OWN, ROWS * PART), jnp.bfloat16),
]
SEMS = pltpu.SemaphoreType.DMA((STEPS,))


def inner_spectra(zh, own, coeffs, table):
    smem, vmem, hbm = (pl.BlockSpec(memory_space=m) for m in (pltpu.SMEM, pltpu.VMEM, pl.ANY))
    partial = (FRAME // 2 // LANES, 2, PART, ROWS, LANES)
    return pl.pallas_call(
        inner_kernel,
        in_specs=[smem, vmem, vmem, hbm],
        out_specs=[hbm, vmem, vmem],
        out_shape=[SPECTRA, pltpu.VMEM(table.shape, table.dtype), pltpu.VMEM(partial, jnp.float32)],
        scratch_shapes=SPECTRA_SCRATCH + [SEMS, SEMS],
        compiler_params=pltpu.CompilerParams(vmem_limit_bytes=20 << 20),
        cost_estimate=pl.CostEstimate(
            flops=2 * CHAN * FRAME * ROWS * PART, bytes_accessed=7 << 20, transcendentals=0
        ),
    )(zh, own, coeffs, pltpu.with_memory_space_constraint(table, pltpu.HBM))


def outer_spectra(zh, prev, following, coeffs, tables, partial, inner):
    smem, vmem, hbm = (pl.BlockSpec(memory_space=m) for m in (pltpu.SMEM, pltpu.VMEM, pl.ANY))
    return pl.pallas_call(
        outer_kernel,
        in_specs=[smem] + [vmem] * 5 + [hbm],
        out_specs=hbm,
        out_shape=SPECTRA,
        scratch_shapes=SPECTRA_SCRATCH + [SEMS],
        input_output_aliases={6: 0},
        compiler_params=pltpu.CompilerParams(vmem_limit_bytes=16 << 20),
        cost_estimate=pl.CostEstimate(
            flops=2 * CHAN * FRAME * ROWS * PART, bytes_accessed=7 << 20, transcendentals=0
        ),
    )(zh, following, prev, coeffs, resident(tables), resident(partial), inner)


def fit(values):
    nodes = (np.cos(np.pi * (np.arange(64) + 0.5) / 64) + 1.0) / 8.0
    return [float(v) for v in np.polynomial.Polynomial.fit(nodes, values(np.sqrt(nodes)), 5, domain=[0, 0.25], window=[0, 0.25]).coef]


COS = fit(lambda r: np.cos(2 * np.pi * r))
SIN = fit(lambda r: np.sin(2 * np.pi * r) / r)


def cos_sin(turns):
    rest = turns - jnp.round(turns)
    square = rest * rest
    cos, sin = COS[-1], SIN[-1]
    for a, b in zip(COS[-2::-1], SIN[-2::-1]):
        cos = cos * square + a
        sin = sin * square + b
    return cos, sin * rest


def input_order():
    order = np.arange(YX * ROWS).reshape(YX, ROWS).transpose(1, 0).reshape(-1)
    return (np.arange(YX * ROWS)[:, None] == order).astype(jnp.bfloat16)


def weights_kernel(first_ref, delays_hbm, order_hbm, out_ref, delays, delays_ref, order_ref, sems):
    copies = [
        pltpu.make_async_copy(delays_hbm, delays_ref, sems.at[0]),
        pltpu.make_async_copy(order_hbm, order_ref, sems.at[1]),
    ]
    for copy in copies:
        copy.start()
    for copy in copies:
        copy.wait()
    block = 128
    size = YX * ROWS

    def reorder(step, carry):
        at = pl.ds(pl.multiple_of(step * block, block), block)
        for group in range(INP):
            cut = slice(group * size, (group + 1) * size)
            rest = delays_ref[at, cut]
            total = jnp.zeros_like(rest)
            for _ in range(3):
                part = rest.astype(jnp.bfloat16)
                rest = rest - part.astype(jnp.float32)
                total = total + jnp.dot(part, order_ref[...], preferred_element_type=jnp.float32)
            delays[at, cut] = total * (1.0 / FRAME)
        return carry

    lax.fori_loop(0, BEAMS // block, reorder, 0)
    block = 16

    def rows(step, carry):
        at = pl.ds(pl.multiple_of(step * block, block), block)
        delay = delays[at]
        step_cos, step_sin = cos_sin(delay)
        cos, sin = cos_sin(delay * first_ref[0])
        for c in range(OWN):
            if c:
                cos, sin = cos * step_cos - sin * step_sin, sin * step_cos + cos * step_sin
            out_ref[c, 0, at] = cos.astype(jnp.bfloat16)
            out_ref[c, 1, at] = (-sin).astype(jnp.bfloat16)
        return carry

    lax.fori_loop(0, BEAMS // block, rows, 0)


def weights(first, delays):
    vmem = pl.BlockSpec(memory_space=pltpu.VMEM)
    return pl.pallas_call(
        weights_kernel,
        in_specs=[pl.BlockSpec(memory_space=m) for m in (pltpu.SMEM, pl.ANY, pl.ANY)],
        out_specs=vmem,
        out_shape=pltpu.VMEM((OWN, 2, BEAMS, INPUTS), jnp.bfloat16),
        scratch_shapes=[
            pltpu.VMEM((BEAMS, INPUTS), jnp.float32),
            pltpu.VMEM((BEAMS, INPUTS), jnp.float32),
            pltpu.VMEM((YX * ROWS, YX * ROWS), jnp.bfloat16),
            pltpu.SemaphoreType.DMA((2,)),
        ],
        compiler_params=pltpu.CompilerParams(vmem_limit_bytes=20 << 20),
        cost_estimate=pl.CostEstimate(
            flops=60 * BEAMS * INPUTS, bytes_accessed=12 << 20, transcendentals=0
        ),
    )(
        first,
        pltpu.with_memory_space_constraint(delays, pltpu.HBM),
        pltpu.with_memory_space_constraint(jnp.asarray(input_order()), pltpu.HBM),
    )


def arrange(wide, own, values):
    place = lax.broadcasted_iota(jnp.int32, (PLACES, LANES), 1) // PART
    rows = 2 * OWN
    halves = ROWS // GROUP
    for half in range(halves):
        for side in range(2):
            row = 4 * (own % 2) + 2 * (own // 2) + side
            a = [
                wide[half + (1 - inner) * halves, pl.ds(zh * PLACES * rows + row, PLACES, stride=rows), :].astype(
                    jnp.bfloat16
                )
                for zh in range(ZH)
                for inner in range(2)
            ]
            for bit in (1, 2, 4):
                moved = place & bit != 0
                a = [jnp.where(moved, a[(k + bit) % GROUP], a[k]) for k in range(GROUP)]
            for k in range(GROUP):
                value = a[-k % GROUP]
                value = pltpu.roll(value, LANES - k * PART, 1) if k else value
                for group in range(INP):
                    at = (group * ROWS + half * GROUP + k) * YX
                    cut = slice(side * LANES, (side + 1) * LANES)
                    values[at : at + YX, cut] = value[group * YX : (group + 1) * YX]


def beams_kernel(spectra_ref, weight, out_ref, wide, values, result, sems):
    for tile in range(ROWS * PLANE // LANES):
        part = spectra_ref[:, :, tile * LANES : (tile + 1) * LANES]
        wide[tile, : DEVICES * 2 * OWN] = part.astype(jnp.float32).reshape(DEVICES * 2 * OWN, LANES)
    lane = lax.broadcasted_iota(jnp.int32, (BEAMS, LANES), 1)
    taken_over = lax.rem(lane, PLANE) < LATE
    copies = []
    for channel in range(OWN):
        arrange(wide, channel, values.at[channel])
        here = values[channel]
        by_re = jnp.dot(weight[channel, 0], here, preferred_element_type=jnp.float32)
        by_im = jnp.dot(weight[channel, 1], here, preferred_element_type=jnp.float32)
        parts = (by_re[:, :LANES] - by_im[:, LANES:], by_re[:, LANES:] + by_im[:, :LANES])
        for side, part in enumerate(parts):
            part = jnp.where(taken_over, pltpu.roll(part, PLANE, 1), part) * (1.0 / math.sqrt(INPUTS))
            result[side, channel] = part.astype(jnp.bfloat16)
        copies.append(pltpu.make_async_copy(result.at[:, channel], out_ref.at[:, channel], sems.at[channel]))
        copies[-1].start()
    for copy in copies:
        copy.wait()


def beams(received, weight):
    vmem = pl.BlockSpec(memory_space=pltpu.VMEM)
    shape = (2, OWN, BEAMS, FRAMES)
    return pl.pallas_call(
        beams_kernel,
        in_specs=[vmem, vmem],
        out_specs=pl.BlockSpec(memory_space=pl.ANY),
        out_shape=jax.ShapeDtypeStruct(shape, jnp.bfloat16),
        scratch_shapes=[
            pltpu.VMEM((ROWS * PLANE // LANES, (DEVICES + 1) * 2 * OWN, LANES), jnp.float32),
            pltpu.VMEM((OWN, INPUTS, 2 * LANES), jnp.bfloat16),
            pltpu.VMEM(shape, jnp.bfloat16),
            pltpu.SemaphoreType.DMA((OWN,)),
        ],
        compiler_params=pltpu.CompilerParams(vmem_limit_bytes=20 << 20),
        cost_estimate=pl.CostEstimate(
            flops=8 * OWN * BEAMS * INPUTS * FRAMES, bytes_accessed=11 << 20, transcendentals=0
        ),
    )(received, resident(weight))


def body(samples, coeffs, delays):
    first = (lax.axis_index(ALL) * OWN).astype(jnp.float32).reshape(1)
    zh = lax.axis_index("zh").astype(jnp.int32).reshape(1)
    table = jnp.asarray(dft_tables())
    up = [(i, i + 1) for i in range(ZH - 1)]
    down = [(i, (i - 1) % ZH) for i in range(ZH)]

    own = lax.all_to_all(samples.reshape(YX, ROWS, 2 * FRAME), ("y", "x"), 0, 0, tiled=True)
    down_frames, up_frames = ends(own)
    following = lax.ppermute(down_frames, "zh", down)
    prev = lax.ppermute(up_frames, "zh", up)
    weight = weights(first, delays)
    inner, tables, partial = inner_spectra(zh, own, coeffs, table)
    following, weight = lax.optimization_barrier((following, weight))
    blocks = outer_spectra(zh, prev, following, coeffs, tables, partial, inner)
    received = lax.all_to_all(blocks, OWNERS, 0, 0, tiled=True)
    return beams(received, weight)


def solution(mesh):
    fine = Mesh(mesh.devices.reshape(4, 4, 4, 2, 2), ALL)
    in_specs = (P(("zl", "core"), ("zh", "y", "x")), P(), P())
    out_specs = P(None, ALL, None, None)
    return jax.shard_map(body, mesh=fine, in_specs=in_specs, out_specs=out_specs, check_vma=False)
```
